128 devices in a mesh: cluster: 8 (over z, core), slab: 16 (over x, y).
Axes of the slice: x: 4, y: 4, z: 4, core: 2. Of those that a mesh axis runs over, the one named last changes fastest.
Arguments:
- queries: bfloat16 [4096, 8, 1024], P(('cluster', 'slab')), may hold values from -30 to 30
- corpus: bfloat16 [128, 1024, 1024], P(('cluster', 'slab')), may hold values from -8 to 8
- block_pairs: int32 [4096, 2], P(('cluster', 'slab')), may hold values from 0 to 127, as said below
- owner_table: int32 [128], replicated, may hold values from 0 to 127, as said below
Outputs:
- shifted: bfloat16 [4096, 8, 1024], P(('cluster', 'slab'))
- log_density: float32 [2, 32768], P(None, ('cluster', 'slab'))
The draws below stay inside these ranges and needn't reach their ends.
Inputs may be any that keep to these rules, and one draw needn't show every extreme that they name: `owner_table`: a permutation: each cluster has its own corpus entry; entry e is held by device e of cluster+slab, so its slab index is e % 16 and its cluster index e // 16. `block_pairs`: the two clusters of a block differ; the 32 blocks of one device name no cluster more than 1 times, and some cluster exactly 1 times; of the 64 clusters named by one device's blocks, exactly 4 are held at each slab index; the blocks of all devices of one cluster index name the cluster of each device exactly 8 times.
All inputs are finite; a program needn't handle non-finite values.
Results may differ from the reference program's by a relative error of at most 0.0046.
Values may be sent and summed in bfloat16 or wider, within the bound.
No kernel may reach another device: no remote copies, remote signals or barrier semaphores. Data moves between devices by JAX's collectives and lax.ppermute only.
A program may use at most 64 MiB of HBM per device.

```python
import jax
import jax.numpy as jnp
from jax import lax

D = 1024
REF_ROWS = 1024
BLOCK = 8
BLK_DEV = 32
STEPS = 2
CLUSTERS = 128
QBLOCKS = 4096
N_CLUSTER = 8
N_SLAB = 16


def routing(key):
    keys = jax.random.split(jax.random.fold_in(key, 101), 2)
    placed = jax.random.permutation(keys[0], CLUSTERS).astype(jnp.int32)
    message_total = 2 * BLK_DEV
    counter = jnp.arange(message_total, dtype=jnp.int32)
    lane = counter % N_SLAB
    turn = counter // N_SLAB
    row_step = (lane + turn) % N_CLUSTER

    def per_row(row_key, row_index):
        first_key, second_key, third_key = jax.random.split(row_key, 3)
        row_perm = jax.random.permutation(first_key, N_CLUSTER).astype(jnp.int32)
        slab_perm = jax.random.permutation(second_key, N_SLAB).astype(jnp.int32)
        source_keys = jax.random.split(third_key, N_SLAB)

        def per_source(source_key, slab_index):
            order_key, flip_key = jax.random.split(source_key)
            target_row = (row_index + row_perm[row_step]) % N_CLUSTER
            target_slab = slab_perm[(slab_index + lane) % N_SLAB]
            entries = (target_row * N_SLAB + target_slab).astype(jnp.int32).reshape(BLK_DEV, 2)
            order = jax.random.permutation(order_key, BLK_DEV)
            entries = entries[order]
            flipped = jax.random.randint(flip_key, (BLK_DEV,), 0, 2) == 1
            left = jnp.where(flipped, entries[:, 1], entries[:, 0])
            right = jnp.where(flipped, entries[:, 0], entries[:, 1])
            return jnp.stack([left, right], axis=1)
        return jax.vmap(per_source)(source_keys, jnp.arange(N_SLAB, dtype=jnp.int32))
    row_keys = jax.random.split(keys[1], N_CLUSTER)
    entries = jax.vmap(per_row)(row_keys, jnp.arange(N_CLUSTER, dtype=jnp.int32)).reshape(QBLOCKS, 2)
    inverse = jnp.argsort(placed).astype(jnp.int32)
    return (placed, inverse[entries].astype(jnp.int32))


def stored_row(key, entry, row_index):
    row_key = jax.random.fold_in(jax.random.fold_in(jax.random.fold_in(key, 202), entry), row_index)
    return jnp.clip(jax.random.normal(row_key, (D,), jnp.float32), -6.0, 6.0)


def draw_owner_table(key, part):
    placed, pairs_drawn = routing(key)
    return placed


def draw_block_pairs(key, part):
    placed, pairs_drawn = routing(key)
    return pairs_drawn


def draw_corpus(key, part):
    entry_ids = jnp.arange(CLUSTERS, dtype=jnp.int32)
    row_ids = jnp.arange(REF_ROWS, dtype=jnp.int32)
    table = jax.vmap(lambda entry: jax.vmap(lambda row_index: stored_row(key, entry, row_index))(row_ids))(entry_ids)
    return table.astype(jnp.bfloat16)


def draw_queries(key, part):
    own_key = jax.random.fold_in(key, 5)
    values = jnp.clip(jax.random.normal(own_key, (QBLOCKS, BLOCK, D), jnp.float32), -6.0, 6.0)
    return values.astype(jnp.bfloat16)


def setup_inputs(seed: int = 0) -> dict:
    key_list = jax.random.split(jax.random.key(seed), 5)
    queries = draw_queries(jax.random.fold_in(key_list[4], 71), 0)
    corpus = draw_corpus(jax.random.fold_in(key_list[4], 71), 0)
    block_pairs = draw_block_pairs(jax.random.fold_in(key_list[4], 71), 0)
    owner_table = draw_owner_table(jax.random.fold_in(key_list[4], 71), 0)
    return dict(queries=queries, corpus=corpus, block_pairs=block_pairs, owner_table=owner_table)


INV_WIDTH = 1.0 / 16.0


def partials(query_rows, cluster_rows, half_norms):
    products = lax.dot_general(query_rows, cluster_rows, (((1,), (1,)), ((), ())), preferred_element_type=jnp.float32)
    scores = (products - half_norms[None, :]) * INV_WIDTH
    row_top = jnp.max(scores, axis=1)
    weights = jnp.exp(scores - row_top[:, None])
    totals = jnp.sum(weights, axis=1)
    summed = jnp.dot(weights.astype(jnp.bfloat16), cluster_rows, preferred_element_type=jnp.float32)
    shifted_part = (summed / totals[:, None]).astype(jnp.bfloat16)
    return shifted_part, row_top + jnp.log(totals)


def combine_pairs(query_rows, first_part, second_part, first_log, second_log):
    both_top = jnp.maximum(first_log, second_log)
    first_share = jnp.exp(first_log - both_top)
    second_share = jnp.exp(second_log - both_top)
    pair_total = first_share + second_share
    mixed = (first_share[:, None] * first_part.astype(jnp.float32) + second_share[:, None] * second_part.astype(jnp.float32)) / pair_total[:, None]
    squares = jnp.sum(jnp.square(query_rows.astype(jnp.float32)), axis=1)
    density = both_top + jnp.log(pair_total) - 0.5 * INV_WIDTH * squares - jnp.log(2.0 * REF_ROWS)
    return mixed.astype(jnp.bfloat16), density


def reference(queries, corpus, block_pairs, owner_table):
    half_norms = 0.5 * jnp.sum(jnp.square(corpus.astype(jnp.float32)), axis=2)
    positions = owner_table[block_pairs]
    current = queries
    densities = []
    for iteration in range(STEPS):
        def one_block(inputs):
            query_rows, places = inputs
            first_part, first_log = partials(query_rows, corpus[places[0]], half_norms[places[0]])
            second_part, second_log = partials(query_rows, corpus[places[1]], half_norms[places[1]])
            return combine_pairs(query_rows, first_part, second_part, first_log, second_log)

        current, density = lax.map(one_block, (current, positions))
        densities.append(density.reshape(-1))
    return current, jnp.stack(densities)
```

```python
import functools
import math

import jax
import jax.numpy as jnp
from jax import lax
from jax.experimental import pallas as pl
from jax.experimental.pallas import tpu as pltpu
from jax.sharding import PartitionSpec as P

STEPS = 2
INV_WIDTH = 1.0 / 16.0
LANES = 128
VMEM_LIMIT = 48 * 1024 * 1024


def whole(space):
    return pl.BlockSpec(memory_space=space)


def params():
    return pltpu.CompilerParams(vmem_limit_bytes=VMEM_LIMIT)


def scatter_kernel(pairs_ref, table_ref, blocks_ref, out_ref):
    def body(block, carry):
        rows = blocks_ref[block]
        out_ref[table_ref[pairs_ref[2 * block]]] = rows
        out_ref[table_ref[pairs_ref[2 * block + 1]]] = rows
        return carry

    lax.fori_loop(0, blocks_ref.shape[0], body, 0, unroll=4)


def scatter_blocks(blocks, pairs, table):
    _, rows, features = blocks.shape
    return pl.pallas_call(
        scatter_kernel,
        out_shape=jax.ShapeDtypeStruct((table.shape[0], rows, features), jnp.bfloat16),
        in_specs=[whole(pltpu.SMEM), whole(pltpu.SMEM), whole(pltpu.VMEM)],
        out_specs=whole(pltpu.VMEM),
        compiler_params=params(),
    )(pairs, table, blocks)


def score_kernel(arrived_ref, cluster_ref, norms_ref, out_ref):
    slots, rows, features = arrived_ref.shape
    cluster = cluster_ref[...]
    flat = arrived_ref[...].astype(jnp.float32).reshape(slots * rows, features).astype(jnp.bfloat16)
    products = lax.dot_general(
        flat, cluster, (((1,), (1,)), ((), ())), preferred_element_type=jnp.float32
    )
    scores = (products - norms_ref[...]) * INV_WIDTH
    row_top = jnp.max(scores, axis=1, keepdims=True)
    weights = jnp.exp(scores - row_top)
    totals = jnp.sum(weights, axis=1, keepdims=True)
    summed = jnp.dot(weights.astype(jnp.bfloat16), cluster, preferred_element_type=jnp.float32)
    part = summed * (1.0 / totals)
    out_ref[:, :, :features] = part.reshape(slots, rows, features).astype(jnp.bfloat16)
    log_weight = row_top + jnp.log(totals)
    first = log_weight.astype(jnp.bfloat16).astype(jnp.float32)
    rest = log_weight - first
    second = rest.astype(jnp.bfloat16).astype(jnp.float32)
    third = rest - second
    lane = lax.broadcasted_iota(jnp.int32, (slots * rows, LANES), 1)
    terms = jnp.where(lane == 0, first, jnp.where(lane == 1, second, third))
    out_ref[:, :, features:] = terms.reshape(slots, rows, LANES).astype(jnp.bfloat16)


def score_slots(arrived, cluster_rows, half_norms, group=32):
    slots, rows, features = arrived.shape
    references = cluster_rows.shape[0]
    return pl.pallas_call(
        score_kernel,
        out_shape=jax.ShapeDtypeStruct((slots, rows, features + LANES), jnp.bfloat16),
        grid=(slots // group,),
        in_specs=[
            pl.BlockSpec((group, rows, features), lambda i: (i, 0, 0)),
            pl.BlockSpec((references, features), lambda i: (0, 0)),
            pl.BlockSpec((1, references), lambda i: (0, 0)),
        ],
        out_specs=pl.BlockSpec((group, rows, features + LANES), lambda i: (i, 0, 0)),
        compiler_params=params(),
    )(arrived, cluster_rows, half_norms)


def combine_kernel(
    log_count, pairs_ref, table_ref, blocks_ref, returned_ref, mixed_ref, density_ref, *send_refs
):
    features = blocks_ref.shape[2]

    def read(slot):
        part = returned_ref[slot].astype(jnp.float32)
        terms = part[:, features:]
        return part[:, :features], terms[:, 0:1] + terms[:, 1:2] + terms[:, 2:3]

    def body(block, carry):
        first_slot = table_ref[pairs_ref[2 * block]]
        second_slot = table_ref[pairs_ref[2 * block + 1]]
        first_part, first_log = read(first_slot)
        second_part, second_log = read(second_slot)
        both_top = jnp.maximum(first_log, second_log)
        first_share = jnp.exp(first_log - both_top)
        second_share = jnp.exp(second_log - both_top)
        pair_total = first_share + second_share
        inverse = 1.0 / pair_total
        mixed = (
            (first_share * inverse) * first_part + (second_share * inverse) * second_part
        ).astype(jnp.bfloat16)
        squares = jnp.sum(
            jnp.square(blocks_ref[block].astype(jnp.float32)), axis=1, keepdims=True
        )
        density = both_top + jnp.log(pair_total) - 0.5 * INV_WIDTH * squares - log_count
        density_ref[block] = jnp.broadcast_to(density, density_ref.shape[1:])
        mixed_ref[block] = mixed
        for send_ref in send_refs:
            send_ref[first_slot] = mixed
            send_ref[second_slot] = mixed
        return carry

    lax.fori_loop(0, blocks_ref.shape[0], body, 0, unroll=4)


def combine(blocks, returned, pairs, table, log_count, send):
    count, rows, features = blocks.shape
    outs = [
        jax.ShapeDtypeStruct(blocks.shape, jnp.bfloat16),
        jax.ShapeDtypeStruct((count, rows, LANES), jnp.float32),
    ]
    if send:
        outs.append(jax.ShapeDtypeStruct((table.shape[0], rows, features), jnp.bfloat16))
    return pl.pallas_call(
        functools.partial(combine_kernel, log_count),
        out_shape=outs,
        in_specs=[whole(pltpu.SMEM), whole(pltpu.SMEM), whole(pltpu.VMEM), whole(pltpu.VMEM)],
        out_specs=[whole(pltpu.VMEM)] * len(outs),
        compiler_params=params(),
    )(pairs, table, blocks, returned)


def exchange(array):
    return lax.all_to_all(array, ("cluster", "slab"), split_axis=0, concat_axis=0, tiled=True)


def local(queries, corpus, block_pairs, owner_table):
    cluster_rows = corpus[0]
    references = cluster_rows.shape[0]
    log_count = math.log(2.0 * references)
    half_norms = 0.5 * jnp.sum(jnp.square(cluster_rows.astype(jnp.float32)), axis=1)[None, :]
    pairs = block_pairs.reshape(-1)
    current = queries
    outgoing = scatter_blocks(current, pairs, owner_table)
    densities = []
    for step in range(STEPS):
        answers = score_slots(exchange(outgoing), cluster_rows, half_norms)
        current, density, *outgoing = combine(
            current, exchange(answers), pairs, owner_table, log_count, step < STEPS - 1
        )
        outgoing = outgoing[0] if outgoing else None
        densities.append(density[:, :, 0].reshape(-1))
    return (current, jnp.stack(densities))


def solution(mesh):
    return jax.shard_map(
        local,
        mesh=mesh,
        in_specs=(
            P(("cluster", "slab"), None, None),
            P(("cluster", "slab"), None, None),
            P(("cluster", "slab"), None),
            P(),
        ),
        out_specs=(P(("cluster", "slab"), None, None), P(None, ("cluster", "slab"))),
        check_vma=False,
    )
```

```python
import functools
import math

import jax
import jax.numpy as jnp
from jax import lax
from jax.experimental import pallas as pl
from jax.experimental.pallas import tpu as pltpu
from jax.sharding import PartitionSpec as P

STEPS = 2
INV_WIDTH = 1.0 / 16.0
LANES = 128
VMEM_LIMIT = 48 * 1024 * 1024
AXES = ("cluster", "slab")
SIDE = 4
CORES = 2
DEPTH = 4
SLABS = SIDE * SIDE
CLUSTER_DEVICES = DEPTH * CORES


def slab_order(core):
    order = [(a, (a + b) % SIDE) for b in range(SIDE) for a in range(SIDE)]
    return [x * SIDE + y if core == 0 else y * SIDE + x for x, y in order]


def slab_groups():
    return [
        [cluster * SLABS + slab for slab in slab_order(cluster % CORES)]
        for cluster in range(CLUSTER_DEVICES)
    ]


def slab_places(core):
    places = [0] * SLABS
    for place, slab in enumerate(slab_order(core)):
        places[slab] = place
    return places


def exchange_slabs(array):
    return lax.all_to_all(
        array, AXES, split_axis=0, concat_axis=0, tiled=True, axis_index_groups=slab_groups()
    )


def shift_depth(array, shift):
    pairs = []
    for z in range(DEPTH):
        for core in range(CORES):
            for slab in range(SLABS):
                source = (z * CORES + core) * SLABS + slab
                target = ((z + shift) % DEPTH * CORES + core) * SLABS + slab
                pairs.append((source, target))
    return lax.ppermute(array, AXES, pairs)


def swap_cores(array):
    pairs = []
    for cluster in range(CLUSTER_DEVICES):
        for slab in range(SLABS):
            pairs.append((cluster * SLABS + slab, (cluster ^ 1) * SLABS + slab))
    return lax.ppermute(array, AXES, pairs)


def whole(space):
    return pl.BlockSpec(memory_space=space)


SMEM, VMEM = whole(pltpu.SMEM), whole(pltpu.VMEM)


def params():
    return pltpu.CompilerParams(vmem_limit_bytes=VMEM_LIMIT)


def fill_kernel(pairs_ref, table_ref, places_ref, blocks_ref, out_ref, slots_ref, counts_ref):
    count, rows, features = blocks_ref.shape
    per_slab = 2 * count // SLABS

    def clear(place, carry):
        counts_ref[place] = 0
        return carry

    lax.fori_loop(0, SLABS, clear, 0)

    def body(block, carry):
        values = blocks_ref[block]
        for side in range(2):
            message = 2 * block + side
            entry = table_ref[pairs_ref[message]]
            place = places_ref[lax.rem(entry, SLABS)]
            rank = counts_ref[place]
            counts_ref[place] = rank + 1
            slot = place * per_slab + rank
            slots_ref[message] = slot
            out_ref[slot, :, :features] = values
            target = lax.div(entry, SLABS).astype(jnp.float32)
            out_ref[slot, :, features:] = jnp.full((rows, LANES), target, jnp.float32).astype(
                jnp.bfloat16
            )
        return carry

    lax.fori_loop(0, count, body, 0, unroll=4)


def fill(blocks, pairs, table, places):
    count, rows, features = blocks.shape
    return pl.pallas_call(
        fill_kernel,
        out_shape=[
            jax.ShapeDtypeStruct((2 * count, rows, features + LANES), jnp.bfloat16),
            jax.ShapeDtypeStruct((2 * count,), jnp.int32),
        ],
        in_specs=[SMEM, SMEM, SMEM, VMEM],
        out_specs=[VMEM, SMEM],
        scratch_shapes=[pltpu.SMEM((SLABS,), jnp.int32)],
        compiler_params=params(),
    )(pairs, table, places, blocks)


def sort_kernel(origin_ref, arrived_ref, *out_refs):
    size, _, features = out_refs[0].shape
    for shift, out_ref in enumerate(out_refs):

        def body(index, carry, shift=shift, out_ref=out_ref):
            out_ref[index] = arrived_ref[origin_ref[shift * size + index], :, :features]
            return carry

        lax.fori_loop(0, size, body, 0, unroll=4)


def sort_by_depth(arrived, origin, features):
    total, rows, _ = arrived.shape
    part = jax.ShapeDtypeStruct((total // DEPTH, rows, features), jnp.bfloat16)
    return pl.pallas_call(
        sort_kernel,
        out_shape=[part] * DEPTH,
        in_specs=[SMEM, VMEM],
        out_specs=[VMEM] * DEPTH,
        compiler_params=params(),
    )(origin, arrived)


def unsort_kernel(origin_ref, *refs):
    part_refs, out_ref = refs[:-1], refs[-1]
    size = part_refs[0].shape[0]
    for shift, part_ref in enumerate(part_refs):

        def body(index, carry, shift=shift, part_ref=part_ref):
            out_ref[origin_ref[shift * size + index]] = part_ref[index]
            return carry

        lax.fori_loop(0, size, body, 0, unroll=4)


def unsort(parts, origin):
    size, rows, width = parts[0].shape
    return pl.pallas_call(
        unsort_kernel,
        out_shape=jax.ShapeDtypeStruct((DEPTH * size, rows, width), jnp.bfloat16),
        in_specs=[SMEM] + [VMEM] * DEPTH,
        out_specs=VMEM,
        compiler_params=params(),
    )(origin, *parts)


def score(flat, cluster, norms):
    products = lax.dot_general(
        flat, cluster, (((1,), (1,)), ((), ())), preferred_element_type=jnp.float32
    )
    scores = (products - norms) * INV_WIDTH
    row_top = jnp.max(scores, axis=1, keepdims=True)
    weights = jnp.exp(scores - row_top)
    totals = jnp.sum(weights, axis=1, keepdims=True)
    summed = jnp.dot(weights.astype(jnp.bfloat16), cluster, preferred_element_type=jnp.float32)
    log_weight = row_top + jnp.log(totals)
    first = log_weight.astype(jnp.bfloat16).astype(jnp.float32)
    rest = log_weight - first
    second = rest.astype(jnp.bfloat16).astype(jnp.float32)
    third = rest - second
    lane = lax.broadcasted_iota(jnp.int32, (flat.shape[0], LANES), 1)
    terms = jnp.where(lane == 0, first, jnp.where(lane == 1, second, third))
    return summed * (1.0 / totals), terms


def score_kernel(*refs):
    part_refs, refs = refs[:DEPTH], refs[DEPTH:]
    cluster_refs, norm_refs, out_refs = refs[:CORES], refs[CORES : 2 * CORES], refs[2 * CORES :]
    size, rows, features = part_refs[0].shape
    half = size // CORES
    for side in range(CORES):
        span = slice(side * half, (side + 1) * half)
        flat = jnp.concatenate(
            [
                part_ref[span].astype(jnp.float32).reshape(half * rows, features)
                for part_ref in part_refs
            ]
        ).astype(jnp.bfloat16)
        part, terms = score(flat, cluster_refs[side][...], norm_refs[side][...])
        for shift, out_ref in enumerate(out_refs):
            lines = slice(shift * half * rows, (shift + 1) * half * rows)
            out_ref[span, :, :features] = (
                part[lines].reshape(half, rows, features).astype(jnp.bfloat16)
            )
            out_ref[span, :, features:] = (
                terms[lines].reshape(half, rows, LANES).astype(jnp.bfloat16)
            )


def score_parts(parts, clusters, norms):
    size, rows, features = parts[0].shape
    out = jax.ShapeDtypeStruct((size, rows, features + LANES), jnp.bfloat16)
    return pl.pallas_call(
        score_kernel,
        out_shape=[out] * DEPTH,
        in_specs=[VMEM] * (DEPTH + 2 * CORES),
        out_specs=[VMEM] * DEPTH,
        compiler_params=params(),
    )(*parts, *clusters, *norms)


def combine_kernel(log_count, slots_ref, blocks_ref, returned_ref, mixed_ref, density_ref, *send_refs):
    features = blocks_ref.shape[2]

    def read(slot):
        part = returned_ref[slot].astype(jnp.float32)
        terms = part[:, features:]
        return part[:, :features], terms[:, 0:1] + terms[:, 1:2] + terms[:, 2:3]

    def body(block, carry):
        first_slot, second_slot = slots_ref[2 * block], slots_ref[2 * block + 1]
        first_part, first_log = read(first_slot)
        second_part, second_log = read(second_slot)
        both_top = jnp.maximum(first_log, second_log)
        first_share = jnp.exp(first_log - both_top)
        second_share = jnp.exp(second_log - both_top)
        pair_total = first_share + second_share
        inverse = 1.0 / pair_total
        mixed = (
            (first_share * inverse) * first_part + (second_share * inverse) * second_part
        ).astype(jnp.bfloat16)
        squares = jnp.sum(
            jnp.square(blocks_ref[block].astype(jnp.float32)), axis=1, keepdims=True
        )
        density = both_top + jnp.log(pair_total) - 0.5 * INV_WIDTH * squares - log_count
        density_ref[block] = jnp.broadcast_to(density, density_ref.shape[1:])
        mixed_ref[block] = mixed
        for send_ref in send_refs:
            send_ref[first_slot] = mixed
            send_ref[second_slot] = mixed
        return carry

    lax.fori_loop(0, blocks_ref.shape[0], body, 0, unroll=4)


def combine(blocks, returned, slots, log_count, send):
    count, rows, features = blocks.shape
    outs = [
        jax.ShapeDtypeStruct(blocks.shape, jnp.bfloat16),
        jax.ShapeDtypeStruct((count, rows, LANES), jnp.float32),
    ]
    if send:
        outs.append(jax.ShapeDtypeStruct((2 * count, rows, features), jnp.bfloat16))
    return pl.pallas_call(
        functools.partial(combine_kernel, log_count),
        out_shape=outs,
        in_specs=[SMEM, VMEM, VMEM],
        out_specs=[VMEM] * len(outs),
        compiler_params=params(),
    )(slots, blocks, returned)


def half_norms_of(cluster_rows):
    return 0.5 * jnp.sum(jnp.square(cluster_rows.astype(jnp.float32)), axis=1)[None, :]


def sorted_origins(arrived, features, depth, core):
    targets = arrived[:, 0, features].astype(jnp.int32)
    total = targets.shape[0]
    per_cluster = total // CLUSTER_DEVICES
    order = jnp.arange(total, dtype=jnp.int32)
    earlier = (targets[:, None] == targets[None, :]) & (order[None, :] < order[:, None])
    rank = jnp.sum(earlier.astype(jnp.int32), axis=1)
    shift = (targets // CORES - depth) % DEPTH
    side = (targets % CORES) ^ core
    slot = (shift * CORES + side) * per_cluster + rank
    return jnp.sum(jnp.where(slot[None, :] == order[:, None], order[None, :], 0), axis=1)


def local(queries, corpus, block_pairs, owner_table):
    features = queries.shape[2]
    cluster_index = lax.axis_index("cluster").astype(jnp.int32)
    depth, core = cluster_index // CORES, cluster_index % CORES
    places = jnp.where(
        core == 0,
        jnp.array(slab_places(0), jnp.int32),
        jnp.array(slab_places(1), jnp.int32),
    )
    own = corpus[0]
    other = swap_cores(own)
    clusters = (own, other)
    norms = (half_norms_of(own), half_norms_of(other))
    log_count = math.log(2.0 * own.shape[0])
    current = queries
    outgoing, slots = fill(current, block_pairs.reshape(-1), owner_table, places)
    origin = None
    densities = []
    for step in range(STEPS):
        arrived = exchange_slabs(outgoing)
        if step == 0:
            origin = sorted_origins(arrived, features, depth, core)
        parts = sort_by_depth(arrived, origin, features)
        parts = [parts[0]] + [shift_depth(parts[k], k) for k in range(1, DEPTH)]
        answers = score_parts(parts, clusters, norms)
        answers = [answers[0]] + [shift_depth(answers[k], -k) for k in range(1, DEPTH)]
        returned = exchange_slabs(unsort(answers, origin))
        current, density, *outgoing = combine(
            current, returned, slots, log_count, step < STEPS - 1
        )
        outgoing = outgoing[0] if outgoing else None
        densities.append(density[:, :, 0].reshape(-1))
    return (current, jnp.stack(densities))


def solution(mesh):
    return jax.shard_map(
        local,
        mesh=mesh,
        in_specs=(
            P(("cluster", "slab"), None, None),
            P(("cluster", "slab"), None, None),
            P(("cluster", "slab"), None),
            P(),
        ),
        out_specs=(P(("cluster", "slab"), None, None), P(None, ("cluster", "slab"))),
        check_vma=False,
    )
```

```python
import functools
import math

import jax
import jax.numpy as jnp
from jax import lax
from jax.experimental import pallas as pl
from jax.experimental.pallas import tpu as pltpu
from jax.sharding import PartitionSpec as P

STEPS = 2
INV_WIDTH = 1.0 / 16.0
LANES = 128
VMEM_LIMIT = 48 * 1024 * 1024
AXES = ("cluster", "slab")
SIDE = 4
CORES = 2
DEPTH = 4
SLABS = SIDE * SIDE
CLUSTER_DEVICES = DEPTH * CORES
SHIFTS = (0, 1, 3, 2)


def slab_order(core):
    order = [(a, (a + b) % SIDE) for b in range(SIDE) for a in range(SIDE)]
    return [x * SIDE + y if core == 0 else y * SIDE + x for x, y in order]


def slab_groups():
    return [
        [cluster * SLABS + slab for slab in slab_order(cluster % CORES)]
        for cluster in range(CLUSTER_DEVICES)
    ]


def exchange_slabs(array):
    return lax.all_to_all(
        array, AXES, split_axis=0, concat_axis=0, tiled=True, axis_index_groups=slab_groups()
    )


def shift_depth(array, shift):
    pairs = []
    for z in range(DEPTH):
        for core in range(CORES):
            for slab in range(SLABS):
                source = (z * CORES + core) * SLABS + slab
                target = ((z + shift) % DEPTH * CORES + core) * SLABS + slab
                pairs.append((source, target))
    return lax.ppermute(array, AXES, pairs)


def swap_cores(array):
    pairs = []
    for cluster in range(CLUSTER_DEVICES):
        for slab in range(SLABS):
            pairs.append((cluster * SLABS + slab, (cluster ^ 1) * SLABS + slab))
    return lax.ppermute(array, AXES, pairs)


def whole(space):
    return pl.BlockSpec(memory_space=space)


SMEM, VMEM = whole(pltpu.SMEM), whole(pltpu.VMEM)


def params():
    return pltpu.CompilerParams(vmem_limit_bytes=VMEM_LIMIT)


def slab_place(slab, core):
    x, y = lax.div(slab, SIDE), lax.rem(slab, SIDE)
    first, second = jnp.where(core == 0, x, y), jnp.where(core == 0, y, x)
    return lax.rem(second - first + SIDE, SIDE) * SIDE + first


def fill_kernel(pairs_ref, table_ref, blocks_ref, out_ref, slots_ref, counts_ref):
    core = lax.rem(lax.axis_index("cluster").astype(jnp.int32), CORES)
    count, rows, features = blocks_ref.shape
    per_slab = 2 * count // SLABS

    def clear(place, carry):
        counts_ref[place] = 0
        return carry

    lax.fori_loop(0, SLABS, clear, 0)

    def body(block, carry):
        values = blocks_ref[block]
        for side in range(2):
            entry = table_ref[pairs_ref[side, block]]
            place = slab_place(lax.rem(entry, SLABS), core)
            rank = counts_ref[place]
            counts_ref[place] = rank + 1
            slot = place * per_slab + rank
            slots_ref[2 * block + side] = slot
            out_ref[slot, :, :features] = values
            target = lax.div(entry, SLABS).astype(jnp.float32)
            out_ref[slot, :, features:] = jnp.full((rows, LANES), target, jnp.float32).astype(
                jnp.bfloat16
            )
        return carry

    lax.fori_loop(0, count, body, 0, unroll=4)


def fill(blocks, pairs, table):
    count, rows, features = blocks.shape
    return pl.pallas_call(
        fill_kernel,
        out_shape=[
            jax.ShapeDtypeStruct((2 * count, rows, features + LANES), jnp.bfloat16),
            jax.ShapeDtypeStruct((2 * count,), jnp.int32),
        ],
        in_specs=[SMEM, SMEM, VMEM],
        out_specs=[VMEM, SMEM],
        scratch_shapes=[pltpu.SMEM((SLABS,), jnp.int32)],
        compiler_params=params(),
    )(pairs, table, blocks)


def sort_kernel(origin_ref, arrived_ref, *out_refs):
    size, _, features = out_refs[0].shape
    for place, out_ref in enumerate(out_refs):

        def body(index, carry, place=place, out_ref=out_ref):
            out_ref[index] = arrived_ref[origin_ref[place * size + index], :, :features]
            return carry

        lax.fori_loop(0, size, body, 0, unroll=4)


def sort_by_depth(arrived, origin, features):
    total, rows, _ = arrived.shape
    part = jax.ShapeDtypeStruct((total // DEPTH, rows, features), jnp.bfloat16)
    return pl.pallas_call(
        sort_kernel,
        out_shape=[part] * DEPTH,
        in_specs=[SMEM, VMEM],
        out_specs=[VMEM] * DEPTH,
        compiler_params=params(),
    )(origin, arrived)


def unsort_kernel(origin_ref, *refs):
    part_refs, out_ref = refs[:-1], refs[-1]
    size = part_refs[0].shape[0]
    for place, part_ref in enumerate(part_refs):

        def body(index, carry, place=place, part_ref=part_ref):
            out_ref[origin_ref[place * size + index]] = part_ref[index]
            return carry

        lax.fori_loop(0, size, body, 0, unroll=4)


def unsort(parts, origin):
    size, rows, width = parts[0].shape
    return pl.pallas_call(
        unsort_kernel,
        out_shape=jax.ShapeDtypeStruct((DEPTH * size, rows, width), jnp.bfloat16),
        in_specs=[SMEM] + [VMEM] * DEPTH,
        out_specs=VMEM,
        compiler_params=params(),
    )(origin, *parts)


def score(flat, cluster, norms):
    products = lax.dot_general(
        flat, cluster, (((1,), (1,)), ((), ())), preferred_element_type=jnp.float32
    )
    scores = (products - norms) * INV_WIDTH
    row_top = jnp.max(scores, axis=1, keepdims=True)
    weights = jnp.exp(scores - row_top)
    totals = jnp.sum(weights, axis=1, keepdims=True)
    summed = jnp.dot(weights.astype(jnp.bfloat16), cluster, preferred_element_type=jnp.float32)
    log_weight = row_top + jnp.log(totals)
    first = log_weight.astype(jnp.bfloat16).astype(jnp.float32)
    rest = log_weight - first
    second = rest.astype(jnp.bfloat16).astype(jnp.float32)
    third = rest - second
    lane = lax.broadcasted_iota(jnp.int32, (flat.shape[0], LANES), 1)
    terms = jnp.where(lane == 0, first, jnp.where(lane == 1, second, third))
    return summed * (1.0 / totals), terms


def score_kernel(count, *refs):
    part_refs, refs = refs[:count], refs[count:]
    cluster_refs, norm_refs, out_refs = refs[:CORES], refs[CORES : 2 * CORES], refs[2 * CORES :]
    size, rows, features = part_refs[0].shape
    half = size // CORES
    for side in range(CORES):
        span = slice(side * half, (side + 1) * half)
        flat = jnp.concatenate(
            [
                part_ref[span].astype(jnp.float32).reshape(half * rows, features)
                for part_ref in part_refs
            ]
        ).astype(jnp.bfloat16)
        part, terms = score(flat, cluster_refs[side][...], norm_refs[side][...])
        for place, out_ref in enumerate(out_refs):
            lines = slice(place * half * rows, (place + 1) * half * rows)
            out_ref[span, :, :features] = (
                part[lines].reshape(half, rows, features).astype(jnp.bfloat16)
            )
            out_ref[span, :, features:] = (
                terms[lines].reshape(half, rows, LANES).astype(jnp.bfloat16)
            )


def score_parts(parts, clusters, norms):
    count = len(parts)
    size, rows, features = parts[0].shape
    references = clusters[0].shape[0]
    total = count * size * rows
    out = jax.ShapeDtypeStruct((size, rows, features + LANES), jnp.bfloat16)
    return pl.pallas_call(
        functools.partial(score_kernel, count),
        out_shape=[out] * count,
        in_specs=[VMEM] * (count + 2 * CORES),
        out_specs=[VMEM] * count,
        compiler_params=params(),
        cost_estimate=pl.CostEstimate(
            flops=4 * total * references * features,
            bytes_accessed=2 * (2 * total * features + CORES * references * features),
            transcendentals=total * references,
        ),
    )(*parts, *clusters, *norms)


def combine_kernel(log_count, slots_ref, blocks_ref, returned_ref, mixed_ref, density_ref, *send_refs):
    features = blocks_ref.shape[2]

    def read(slot):
        part = returned_ref[slot].astype(jnp.float32)
        terms = part[:, features:]
        return part[:, :features], terms[:, 0:1] + terms[:, 1:2] + terms[:, 2:3]

    def body(block, densities):
        first_slot, second_slot = slots_ref[2 * block], slots_ref[2 * block + 1]
        first_part, first_log = read(first_slot)
        second_part, second_log = read(second_slot)
        both_top = jnp.maximum(first_log, second_log)
        first_share = jnp.exp(first_log - both_top)
        second_share = jnp.exp(second_log - both_top)
        pair_total = first_share + second_share
        inverse = 1.0 / pair_total
        mixed = (
            (first_share * inverse) * first_part + (second_share * inverse) * second_part
        ).astype(jnp.bfloat16)
        squares = jnp.sum(
            jnp.square(blocks_ref[block].astype(jnp.float32)), axis=1, keepdims=True
        )
        density = both_top + jnp.log(pair_total) - 0.5 * INV_WIDTH * squares - log_count
        mixed_ref[block] = mixed
        for send_ref in send_refs:
            send_ref[first_slot] = mixed
            send_ref[second_slot] = mixed
        return jnp.where(lane == block, density, densities)

    lane = lax.broadcasted_iota(jnp.int32, density_ref.shape, 1)
    density_ref[...] = lax.fori_loop(
        0, blocks_ref.shape[0], body, jnp.zeros(density_ref.shape, jnp.float32), unroll=4
    )


def combine(blocks, returned, slots, log_count, send):
    count, rows, features = blocks.shape
    outs = [
        jax.ShapeDtypeStruct(blocks.shape, jnp.bfloat16),
        jax.ShapeDtypeStruct((rows, LANES), jnp.float32),
    ]
    if send:
        outs.append(jax.ShapeDtypeStruct((2 * count, rows, features), jnp.bfloat16))
    return pl.pallas_call(
        functools.partial(combine_kernel, log_count),
        out_shape=outs,
        in_specs=[SMEM, VMEM, VMEM],
        out_specs=[VMEM] * len(outs),
        compiler_params=params(),
    )(slots, blocks, returned)


def half_norms_of(cluster_rows):
    return 0.5 * jnp.sum(jnp.square(cluster_rows.astype(jnp.float32)), axis=1)[None, :]


def sorted_origins(arrived, features, depth, core):
    targets = arrived[:, 0, features].astype(jnp.int32)
    total = targets.shape[0]
    per_cluster = total // CLUSTER_DEVICES
    order = jnp.arange(total, dtype=jnp.int32)
    earlier = (targets[:, None] == targets[None, :]) & (order[None, :] < order[:, None])
    rank = jnp.sum(earlier.astype(jnp.int32), axis=1)
    shift = (targets // CORES - depth) % DEPTH
    place = shift ^ (shift >> 1)
    side = (targets % CORES) ^ core
    slot = (place * CORES + side) * per_cluster + rank
    return jnp.sum(jnp.where(slot[None, :] == order[:, None], order[None, :], 0), axis=1)


def local(queries, corpus, block_pairs, owner_table):
    features = queries.shape[2]
    cluster_index = lax.axis_index("cluster").astype(jnp.int32)
    depth, core = cluster_index // CORES, cluster_index % CORES
    own = corpus[0]
    other = swap_cores(own)
    clusters = (own, other)
    norms = (half_norms_of(own), half_norms_of(other))
    log_count = math.log(2.0 * own.shape[0])
    current = queries
    outgoing, slots = fill(current, block_pairs.T, owner_table)
    origin = None
    densities = []
    for step in range(STEPS):
        arrived = exchange_slabs(outgoing)
        if step == 0:
            origin = sorted_origins(arrived, features, depth, core)
        parts = sort_by_depth(arrived, origin, features)
        parts = [parts[0]] + [shift_depth(p, k) for p, k in zip(parts[1:], SHIFTS[1:])]
        answers = score_parts(parts[:-1], clusters, norms)
        last, _ = lax.optimization_barrier((parts[-1], answers[0]))
        answers += score_parts([last], clusters, norms)
        answers = [answers[0]] + [shift_depth(a, -k) for a, k in zip(answers[1:], SHIFTS[1:])]
        returned = exchange_slabs(unsort(answers, origin))
        current, density, *outgoing = combine(
            current, returned, slots, log_count, step < STEPS - 1
        )
        outgoing = outgoing[0] if outgoing else None
        densities.append(density[:, : queries.shape[0]].T.reshape(-1))
    return (current, jnp.stack(densities))


def solution(mesh):
    return jax.shard_map(
        local,
        mesh=mesh,
        in_specs=(
            P(("cluster", "slab"), None, None),
            P(("cluster", "slab"), None, None),
            P(("cluster", "slab"), None),
            P(),
        ),
        out_specs=(P(("cluster", "slab"), None, None), P(None, ("cluster", "slab"))),
        check_vma=False,
    )
```

```python
import functools
import math

import jax
import jax.numpy as jnp
from jax import lax
from jax.experimental import pallas as pl
from jax.experimental.pallas import tpu as pltpu
from jax.sharding import PartitionSpec as P

STEPS = 2
INV_WIDTH = 1.0 / 16.0
LANES = 128
VMEM_LIMIT = 48 * 1024 * 1024
AXES = ("cluster", "slab")
SIDE = 4
CORES = 2
DEPTH = 4
SLABS = SIDE * SIDE
CLUSTER_DEVICES = DEPTH * CORES
SHIFTS = (0, 1, 3, 2)
TERM_LANES = 8


def slab_order(core):
    order = [(a, (a + b) % SIDE) for b in range(SIDE) for a in range(SIDE)]
    return [x * SIDE + y if core == 0 else y * SIDE + x for x, y in order]


def slab_groups():
    return [
        [cluster * SLABS + slab for slab in slab_order(cluster % CORES)]
        for cluster in range(CLUSTER_DEVICES)
    ]


def exchange_slabs(array):
    return lax.all_to_all(
        array, AXES, split_axis=0, concat_axis=0, tiled=True, axis_index_groups=slab_groups()
    )


def shift_depth(array, shift):
    pairs = []
    for z in range(DEPTH):
        for core in range(CORES):
            for slab in range(SLABS):
                source = (z * CORES + core) * SLABS + slab
                target = ((z + shift) % DEPTH * CORES + core) * SLABS + slab
                pairs.append((source, target))
    return lax.ppermute(array, AXES, pairs)


def swap_cores(array):
    pairs = []
    for cluster in range(CLUSTER_DEVICES):
        for slab in range(SLABS):
            pairs.append((cluster * SLABS + slab, (cluster ^ 1) * SLABS + slab))
    return lax.ppermute(array, AXES, pairs)


def whole(space):
    return pl.BlockSpec(memory_space=space)


SMEM, VMEM = whole(pltpu.SMEM), whole(pltpu.VMEM)


def params():
    return pltpu.CompilerParams(vmem_limit_bytes=VMEM_LIMIT)


def slab_place(slab, core):
    x, y = lax.div(slab, SIDE), lax.rem(slab, SIDE)
    first, second = jnp.where(core == 0, x, y), jnp.where(core == 0, y, x)
    return lax.rem(second - first + SIDE, SIDE) * SIDE + first


def fill_kernel(
    pairs_hbm, table_hbm, blocks_ref, out_ref, slots_ref,
    pairs_ref, table_ref, counts_ref, targets_ref, notes_ref, input_sems, copy_sems, note_sem,
):
    count, tiles = blocks_ref.shape[:2]
    per_slab = 2 * count // SLABS
    core = lax.rem(lax.axis_index("cluster").astype(jnp.int32), CORES)
    inputs = [
        pltpu.make_async_copy(pairs_hbm, pairs_ref, input_sems.at[0]),
        pltpu.make_async_copy(table_hbm, table_ref, input_sems.at[1]),
    ]
    for copy in inputs:
        copy.start()

    def clear(place, carry):
        counts_ref[place] = 0
        return carry

    lax.fori_loop(0, SLABS, clear, 0)
    for copy in inputs:
        copy.wait()

    def message_copy(message, slot):
        place, rank = lax.div(slot, per_slab), lax.rem(slot, per_slab)
        return pltpu.make_async_copy(
            blocks_ref.at[lax.div(message, 2)],
            out_ref.at[place, pl.ds(rank * tiles, tiles)],
            copy_sems.at[message],
        )

    def send(block, carry):
        for side in range(2):
            entry = table_ref[pairs_ref[side, block]]
            place = slab_place(lax.rem(entry, SLABS), core)
            rank = counts_ref[place]
            counts_ref[place] = rank + 1
            slot = place * per_slab + rank
            message = 2 * block + side
            slots_ref[message] = slot
            targets_ref[slot] = lax.div(entry, SLABS)
            message_copy(message, slot).start()
        return carry

    lax.fori_loop(0, count, send, 0, unroll=2)
    lane = lax.broadcasted_iota(jnp.int32, notes_ref.shape[1:], 1)

    def note(place, carry):
        tile = jnp.zeros(notes_ref.shape[1:], jnp.int32)
        for rank in range(per_slab):
            tile = jnp.where(lane == rank, targets_ref[place * per_slab + rank], tile)
        notes_ref[place] = tile.astype(jnp.float32).astype(jnp.bfloat16)
        return carry

    lax.fori_loop(0, SLABS, note, 0, unroll=2)
    note_copy = pltpu.make_async_copy(notes_ref, out_ref.at[:, per_slab * tiles], note_sem)
    note_copy.start()

    def wait(message, carry):
        message_copy(message, slots_ref[message]).wait()
        return carry

    lax.fori_loop(0, 2 * count, wait, 0, unroll=2)
    note_copy.wait()


def fill(blocks, pairs, table):
    count, rows, features = blocks.shape
    tiles = features // LANES
    chunk = 2 * count // SLABS * tiles + 1
    tiled = blocks.reshape(count, rows, tiles, LANES).transpose(0, 2, 1, 3)
    hbm = whole(pltpu.HBM)
    out, slots = pl.pallas_call(
        fill_kernel,
        out_shape=[
            jax.ShapeDtypeStruct((SLABS, chunk, rows, LANES), jnp.bfloat16),
            jax.ShapeDtypeStruct((2 * count,), jnp.int32),
        ],
        in_specs=[hbm, hbm, hbm],
        out_specs=[hbm, SMEM],
        scratch_shapes=[
            pltpu.SMEM(pairs.shape, jnp.int32),
            pltpu.SMEM(table.shape, jnp.int32),
            pltpu.SMEM((SLABS,), jnp.int32),
            pltpu.SMEM((2 * count,), jnp.int32),
            pltpu.VMEM((SLABS, rows, LANES), jnp.bfloat16),
            pltpu.SemaphoreType.DMA((2,)),
            pltpu.SemaphoreType.DMA((2 * count,)),
            pltpu.SemaphoreType.DMA,
        ],
        compiler_params=params(),
    )(pairs, table, tiled)
    return out.reshape(SLABS * chunk, rows, LANES), slots


def chunk_base(message, per_slab, tiles):
    place, rank = lax.div(message, per_slab), lax.rem(message, per_slab)
    first = place * (per_slab * tiles + 1)
    return first + rank * tiles, first + per_slab * tiles, rank


def sort_kernel(origin_ref, arrived_ref, *out_refs):
    size, _, features = out_refs[0].shape
    tiles = features // LANES
    per_slab = DEPTH * size // SLABS
    chunked = arrived_ref.shape[2] != features
    for place, out_ref in enumerate(out_refs):

        def body(index, carry, place=place, out_ref=out_ref):
            origin = origin_ref[place * size + index]
            if not chunked:
                out_ref[index] = arrived_ref[origin]
                return carry
            base, _, _ = chunk_base(origin, per_slab, tiles)
            for tile in range(tiles):
                out_ref[index, :, tile * LANES : (tile + 1) * LANES] = arrived_ref[base + tile]
            return carry

        lax.fori_loop(0, size, body, 0, unroll=4)


def sort_by_depth(arrived, origin, features):
    total, rows = origin.shape[0], arrived.shape[1]
    part = jax.ShapeDtypeStruct((total // DEPTH, rows, features), jnp.bfloat16)
    return pl.pallas_call(
        sort_kernel,
        out_shape=[part] * DEPTH,
        in_specs=[SMEM, VMEM],
        out_specs=[VMEM] * DEPTH,
        compiler_params=params(),
    )(origin, arrived)


def unsort_kernel(origin_ref, *refs):
    part_refs, out_ref, logs_ref = refs[:DEPTH], refs[DEPTH], refs[DEPTH + 1]
    size, _, features = part_refs[0].shape
    size -= 1
    tiles = features // LANES
    total = DEPTH * size
    per_slab = total // SLABS
    for place, part_ref in enumerate(part_refs):
        terms = part_ref[size, :, :LANES].astype(jnp.float32)

        def body(index, carry, place=place, part_ref=part_ref, terms=terms):
            origin = origin_ref[place * size + index]
            base, _, rank = chunk_base(origin, per_slab, tiles)
            for tile in range(tiles):
                out_ref[base + tile] = part_ref[index, :, tile * LANES : (tile + 1) * LANES]
            shift = lax.rem((rank - index) * TERM_LANES + LANES, LANES)
            logs_ref[origin] = pltpu.roll(terms, shift, 1)
            return carry

        lax.fori_loop(0, size, body, 0, unroll=4)
    lane = lax.broadcasted_iota(jnp.int32, logs_ref.shape[1:], 1) // TERM_LANES

    def pack(place, carry):
        tile = logs_ref[place * per_slab]
        for rank in range(1, per_slab):
            tile = jnp.where(lane == rank, logs_ref[place * per_slab + rank], tile)
        out_ref[place * (per_slab * tiles + 1) + per_slab * tiles] = tile.astype(jnp.bfloat16)
        return carry

    lax.fori_loop(0, SLABS, pack, 0, unroll=2)


def unsort(parts, origin):
    size, rows, features = parts[0].shape
    total = origin.shape[0]
    chunk = total // SLABS * (features // LANES) + 1
    return pl.pallas_call(
        unsort_kernel,
        out_shape=jax.ShapeDtypeStruct((SLABS * chunk, rows, LANES), jnp.bfloat16),
        in_specs=[SMEM] + [VMEM] * DEPTH,
        out_specs=VMEM,
        scratch_shapes=[pltpu.VMEM((total, rows, LANES), jnp.float32)],
        compiler_params=params(),
    )(origin, *parts)


def score(flat, cluster, norms):
    products = lax.dot_general(
        flat, cluster, (((1,), (1,)), ((), ())), preferred_element_type=jnp.float32
    )
    scores = (products - norms) * INV_WIDTH
    row_top = jnp.max(scores, axis=1, keepdims=True)
    weights = jnp.exp(scores - row_top)
    totals = jnp.sum(weights, axis=1, keepdims=True)
    summed = jnp.dot(weights.astype(jnp.bfloat16), cluster, preferred_element_type=jnp.float32)
    log_weight = row_top + jnp.log(totals)
    first = log_weight.astype(jnp.bfloat16).astype(jnp.float32)
    rest = log_weight - first
    second = rest.astype(jnp.bfloat16).astype(jnp.float32)
    third = rest - second
    lane = lax.broadcasted_iota(jnp.int32, (flat.shape[0], LANES), 1) % TERM_LANES
    terms = jnp.where(lane == 0, first, jnp.where(lane == 1, second, third))
    return summed * (1.0 / totals), terms


def score_kernel(*refs):
    part_refs, refs = refs[:DEPTH], refs[DEPTH:]
    cluster_refs, norm_refs, out_refs = refs[:CORES], refs[CORES : 2 * CORES], refs[2 * CORES :]
    size, rows, features = part_refs[0].shape
    half = size // CORES
    lane = lax.broadcasted_iota(jnp.int32, (rows, LANES), 1) // TERM_LANES
    shared = [jnp.zeros((rows, LANES), jnp.float32)] * DEPTH
    for side in range(CORES):
        span = slice(side * half, (side + 1) * half)
        flat = jnp.concatenate(
            [
                part_ref[span].astype(jnp.float32).reshape(half * rows, features)
                for part_ref in part_refs
            ]
        ).astype(jnp.bfloat16)
        part, terms = score(flat, cluster_refs[side][...], norm_refs[side][...])
        for place, out_ref in enumerate(out_refs):
            first = place * half * rows
            lines = part[first : first + half * rows]
            out_ref[span] = lines.reshape(half, rows, features).astype(jnp.bfloat16)
            for index in range(half):
                line = first + index * rows
                shared[place] = jnp.where(
                    lane == side * half + index, terms[line : line + rows], shared[place]
                )
    for place, out_ref in enumerate(out_refs):
        out_ref[size, :, :LANES] = shared[place].astype(jnp.bfloat16)


def score_parts(parts, clusters, norms):
    size, rows, features = parts[0].shape
    references = clusters[0].shape[0]
    total = DEPTH * size * rows
    out = jax.ShapeDtypeStruct((size + 1, rows, features), jnp.bfloat16)
    return pl.pallas_call(
        score_kernel,
        out_shape=[out] * DEPTH,
        in_specs=[VMEM] * (DEPTH + 2 * CORES),
        out_specs=[VMEM] * DEPTH,
        compiler_params=params(),
        cost_estimate=pl.CostEstimate(
            flops=4 * total * references * features,
            bytes_accessed=2 * (2 * total * features + CORES * references * features),
            transcendentals=total * references,
        ),
    )(*parts, *clusters, *norms)


def combine_kernel(log_count, slots_ref, blocks_ref, returned_ref, mixed_ref, density_ref, *send_refs):
    count, _, features = blocks_ref.shape
    tiles = features // LANES
    per_slab = 2 * count // SLABS

    def read(slot):
        base, last, rank = chunk_base(slot, per_slab, tiles)
        part = returned_ref[pl.ds(base, tiles)].astype(jnp.float32)
        terms = returned_ref[last].astype(jnp.float32)
        terms = pltpu.roll(terms, lax.rem(LANES - rank * TERM_LANES, LANES), 1)
        return part, terms[:, 0:1] + terms[:, 1:2] + terms[:, 2:3]

    def body(block, densities):
        first_slot, second_slot = slots_ref[2 * block], slots_ref[2 * block + 1]
        first_part, first_log = read(first_slot)
        second_part, second_log = read(second_slot)
        both_top = jnp.maximum(first_log, second_log)
        first_share = jnp.exp(first_log - both_top)
        second_share = jnp.exp(second_log - both_top)
        pair_total = first_share + second_share
        inverse = 1.0 / pair_total
        mixed = (
            (first_share * inverse)[None] * first_part
            + (second_share * inverse)[None] * second_part
        ).astype(jnp.bfloat16)
        squares = jnp.sum(
            jnp.square(blocks_ref[block].astype(jnp.float32)), axis=1, keepdims=True
        )
        density = both_top + jnp.log(pair_total) - 0.5 * INV_WIDTH * squares - log_count
        for tile in range(tiles):
            lanes = slice(tile * LANES, (tile + 1) * LANES)
            mixed_ref[block, :, lanes] = mixed[tile]
            for send_ref in send_refs:
                send_ref[first_slot, :, lanes] = mixed[tile]
                send_ref[second_slot, :, lanes] = mixed[tile]
        return jnp.where(lane == block, density, densities)

    lane = lax.broadcasted_iota(jnp.int32, density_ref.shape, 1)
    density_ref[...] = lax.fori_loop(
        0, blocks_ref.shape[0], body, jnp.zeros(density_ref.shape, jnp.float32), unroll=4
    )


def combine(blocks, returned, slots, log_count, send):
    count, rows, features = blocks.shape
    outs = [
        jax.ShapeDtypeStruct(blocks.shape, jnp.bfloat16),
        jax.ShapeDtypeStruct((rows, LANES), jnp.float32),
    ]
    if send:
        outs.append(jax.ShapeDtypeStruct((2 * count, rows, features), jnp.bfloat16))
    return pl.pallas_call(
        functools.partial(combine_kernel, log_count),
        out_shape=outs,
        in_specs=[SMEM, VMEM, VMEM],
        out_specs=[VMEM] * len(outs),
        compiler_params=params(),
    )(slots, blocks, returned)


def half_norms_of(cluster_rows):
    return 0.5 * jnp.sum(jnp.square(cluster_rows.astype(jnp.float32)), axis=1)[None, :]


def sorted_origins(arrived, total, depth, core):
    chunks = arrived.reshape(SLABS, -1, *arrived.shape[1:])
    targets = chunks[:, -1, 0, : total // SLABS].reshape(-1).astype(jnp.int32)
    per_cluster = total // CLUSTER_DEVICES
    order = jnp.arange(total, dtype=jnp.int32)
    earlier = (targets[:, None] == targets[None, :]) & (order[None, :] < order[:, None])
    rank = jnp.sum(earlier.astype(jnp.int32), axis=1)
    shift = (targets // CORES - depth) % DEPTH
    place = shift ^ (shift >> 1)
    side = (targets % CORES) ^ core
    slot = (place * CORES + side) * per_cluster + rank
    return jnp.sum(jnp.where(slot[None, :] == order[:, None], order[None, :], 0), axis=1)


def local(queries, corpus, block_pairs, owner_table):
    features = queries.shape[2]
    cluster_index = lax.axis_index("cluster").astype(jnp.int32)
    depth, core = cluster_index // CORES, cluster_index % CORES
    own = corpus[0]
    other = swap_cores(own)
    clusters = (own, other)
    norms = (half_norms_of(own), half_norms_of(other))
    log_count = math.log(2.0 * own.shape[0])
    current = queries
    outgoing, slots = fill(current, block_pairs.T, owner_table)
    origin = None
    densities = []
    for step in range(STEPS):
        arrived = exchange_slabs(outgoing)
        if step == 0:
            origin = sorted_origins(arrived, slots.shape[0], depth, core)
        parts = sort_by_depth(arrived, origin, features)
        parts = [parts[0]] + [shift_depth(p, k) for p, k in zip(parts[1:], SHIFTS[1:])]
        answers = score_parts(parts, clusters, norms)
        answers = [answers[0]] + [shift_depth(a, -k) for a, k in zip(answers[1:], SHIFTS[1:])]
        returned = exchange_slabs(unsort(answers, origin))
        current, density, *outgoing = combine(
            current, returned, slots, log_count, step < STEPS - 1
        )
        outgoing = outgoing[0] if outgoing else None
        densities.append(density[:, : queries.shape[0]].T.reshape(-1))
    return (current, jnp.stack(densities))


def solution(mesh):
    return jax.shard_map(
        local,
        mesh=mesh,
        in_specs=(
            P(("cluster", "slab"), None, None),
            P(("cluster", "slab"), None, None),
            P(("cluster", "slab"), None),
            P(),
        ),
        out_specs=(P(("cluster", "slab"), None, None), P(None, ("cluster", "slab"))),
        check_vma=False,
    )
```

```python
import functools
import math

import jax
import jax.numpy as jnp
from jax import lax
from jax.experimental import pallas as pl
from jax.experimental.pallas import tpu as pltpu
from jax.sharding import PartitionSpec as P

STEPS = 2
INV_WIDTH = 1.0 / 16.0
LANES = 128
VMEM_LIMIT = 48 * 1024 * 1024
AXES = ("cluster", "slab")
SIDE = 4
CORES = 2
DEPTH = 4
SLABS = SIDE * SIDE
CLUSTER_DEVICES = DEPTH * CORES
SHIFTS = (0, 1, 3, 2)
TERM_LANES = 8
TERMS = 3


def slab_order(core):
    order = [(a, (a + b) % SIDE) for b in range(SIDE) for a in range(SIDE)]
    return [x * SIDE + y if core == 0 else y * SIDE + x for x, y in order]


def slab_groups():
    return [
        [cluster * SLABS + slab for slab in slab_order(cluster % CORES)]
        for cluster in range(CLUSTER_DEVICES)
    ]


def exchange_slabs(array):
    return lax.all_to_all(
        array, AXES, split_axis=0, concat_axis=0, tiled=True, axis_index_groups=slab_groups()
    )


def shift_depth(array, shift):
    pairs = []
    for z in range(DEPTH):
        for core in range(CORES):
            for slab in range(SLABS):
                source = (z * CORES + core) * SLABS + slab
                target = ((z + shift) % DEPTH * CORES + core) * SLABS + slab
                pairs.append((source, target))
    return lax.ppermute(array, AXES, pairs)


def swap_cores(array):
    pairs = []
    for cluster in range(CLUSTER_DEVICES):
        for slab in range(SLABS):
            pairs.append((cluster * SLABS + slab, (cluster ^ 1) * SLABS + slab))
    return lax.ppermute(array, AXES, pairs)


def whole(space):
    return pl.BlockSpec(memory_space=space)


SMEM, VMEM = whole(pltpu.SMEM), whole(pltpu.VMEM)


def params():
    return pltpu.CompilerParams(vmem_limit_bytes=VMEM_LIMIT)


def slab_place(slab, core):
    x, y = lax.div(slab, SIDE), lax.rem(slab, SIDE)
    first, second = jnp.where(core == 0, x, y), jnp.where(core == 0, y, x)
    return lax.rem(second - first + SIDE, SIDE) * SIDE + first


def fill_kernel(
    pairs_hbm, table_hbm, blocks_ref, out_ref, slots_ref,
    pairs_ref, table_ref, counts_ref, targets_ref, input_sems,
):
    count, rows, features = blocks_ref.shape
    tiles = features // LANES
    per_slab = 2 * count // SLABS
    core = lax.rem(lax.axis_index("cluster").astype(jnp.int32), CORES)
    inputs = [
        pltpu.make_async_copy(pairs_hbm, pairs_ref, input_sems.at[0]),
        pltpu.make_async_copy(table_hbm, table_ref, input_sems.at[1]),
    ]
    for copy in inputs:
        copy.start()
    for place in range(SLABS):
        counts_ref[place] = 0
    for copy in inputs:
        copy.wait()

    def assign(block, carry):
        for side in range(2):
            entry = table_ref[pairs_ref[side, block]]
            place = slab_place(lax.rem(entry, SLABS), core)
            rank = counts_ref[place]
            counts_ref[place] = rank + 1
            slot = place * per_slab + rank
            slots_ref[2 * block + side] = slot
            targets_ref[slot] = lax.div(entry, SLABS)
        return carry

    lax.fori_loop(0, count, assign, 0, unroll=4)

    def put(block, carry):
        bases = [chunk_base(slots_ref[2 * block + side], per_slab, tiles)[0] for side in range(2)]
        for tile in range(tiles):
            values = blocks_ref[block, :, tile * LANES : (tile + 1) * LANES]
            for base in bases:
                out_ref[base + tile] = values
        return carry

    lax.fori_loop(0, count, put, 0, unroll=4)
    lane = lax.broadcasted_iota(jnp.int32, (rows, LANES), 1)

    def note(place, carry):
        tile = jnp.zeros((rows, LANES), jnp.int32)
        for rank in range(per_slab):
            tile = jnp.where(lane == rank, targets_ref[place * per_slab + rank], tile)
        tile = tile.astype(jnp.float32).astype(jnp.bfloat16)
        out_ref[place * (per_slab * tiles + 1) + per_slab * tiles] = tile
        return carry

    lax.fori_loop(0, SLABS, note, 0, unroll=4)


def fill(blocks, pairs, table):
    count, rows, features = blocks.shape
    chunk = 2 * count // SLABS * (features // LANES) + 1
    pairs = pltpu.with_memory_space_constraint(pairs, pltpu.HBM)
    table = pltpu.with_memory_space_constraint(table, pltpu.HBM)
    hbm = whole(pltpu.HBM)
    return pl.pallas_call(
        fill_kernel,
        out_shape=[
            jax.ShapeDtypeStruct((SLABS * chunk, rows, LANES), jnp.bfloat16),
            jax.ShapeDtypeStruct((2 * count,), jnp.int32),
        ],
        in_specs=[hbm, hbm, VMEM],
        out_specs=[VMEM, SMEM],
        scratch_shapes=[
            pltpu.SMEM(pairs.shape, jnp.int32),
            pltpu.SMEM(table.shape, jnp.int32),
            pltpu.SMEM((SLABS,), jnp.int32),
            pltpu.SMEM((2 * count,), jnp.int32),
            pltpu.SemaphoreType.DMA((2,)),
        ],
        compiler_params=params(),
    )(pairs, table, blocks)


def chunk_base(message, per_slab, tiles):
    place, rank = lax.div(message, per_slab), lax.rem(message, per_slab)
    first = place * (per_slab * tiles + 1)
    return first + rank * tiles, first + per_slab * tiles, rank


def sort_kernel(origin_ref, arrived_ref, *out_refs):
    size, _, features = out_refs[0].shape
    tiles = features // LANES
    per_slab = DEPTH * size // SLABS
    chunked = arrived_ref.shape[2] != features
    for place, out_ref in enumerate(out_refs):

        def body(index, carry, place=place, out_ref=out_ref):
            origin = origin_ref[place * size + index]
            if not chunked:
                out_ref[index] = arrived_ref[origin]
                return carry
            base, _, _ = chunk_base(origin, per_slab, tiles)
            for tile in range(tiles):
                out_ref[index, :, tile * LANES : (tile + 1) * LANES] = arrived_ref[base + tile]
            return carry

        lax.fori_loop(0, size, body, 0, unroll=4)


def sort_by_depth(arrived, origin, features):
    total, rows = origin.shape[0], arrived.shape[1]
    part = jax.ShapeDtypeStruct((total // DEPTH, rows, features), jnp.bfloat16)
    return pl.pallas_call(
        sort_kernel,
        out_shape=[part] * DEPTH,
        in_specs=[SMEM, VMEM],
        out_specs=[VMEM] * DEPTH,
        compiler_params=params(),
    )(origin, arrived)


def unsort_kernel(origin_ref, *refs):
    part_refs, out_ref, logs_ref = refs[:DEPTH], refs[DEPTH], refs[DEPTH + 1]
    size, rows, features = part_refs[0].shape
    size -= 1
    tiles = features // LANES
    total = DEPTH * size
    per_slab = total // SLABS
    lane = lax.broadcasted_iota(jnp.int32, (rows, LANES), 1)
    halves = [lane < LANES // 2, lane >= LANES // 2]
    for place, part_ref in enumerate(part_refs):
        for index in range(size):
            origin = origin_ref[place * size + index]
            base, _, _ = chunk_base(origin, per_slab, tiles)
            for tile in range(tiles):
                out_ref[base + tile] = part_ref[index, :, tile * LANES : (tile + 1) * LANES]
            first = index // 2 * LANES
            terms = part_ref[size, :, first : first + LANES].astype(jnp.float32)
            logs_ref[origin] = jnp.where(halves[index % 2], terms, 0.0)
    slot = lane % (LANES // 2) // TERM_LANES

    def pack(place, carry):
        tile = logs_ref[place * per_slab]
        for rank in range(1, per_slab):
            tile = jnp.where(slot == rank, logs_ref[place * per_slab + rank], tile)
        out_ref[place * (per_slab * tiles + 1) + per_slab * tiles] = tile.astype(jnp.bfloat16)
        return carry

    lax.fori_loop(0, SLABS, pack, 0, unroll=4)


def unsort(parts, origin):
    size, rows, features = parts[0].shape
    total = origin.shape[0]
    chunk = total // SLABS * (features // LANES) + 1
    return pl.pallas_call(
        unsort_kernel,
        out_shape=jax.ShapeDtypeStruct((SLABS * chunk, rows, LANES), jnp.bfloat16),
        in_specs=[SMEM] + [VMEM] * DEPTH,
        out_specs=VMEM,
        scratch_shapes=[pltpu.VMEM((total, rows, LANES), jnp.float32)],
        compiler_params=params(),
    )(origin, *parts)


def score(flat, cluster, norms):
    products = lax.dot_general(
        flat, cluster, (((1,), (1,)), ((), ())), preferred_element_type=jnp.float32
    )
    scores = (products - norms) * INV_WIDTH
    row_top = jnp.max(scores, axis=1, keepdims=True)
    weights = jnp.exp(scores - row_top)
    totals = jnp.sum(weights, axis=1, keepdims=True)
    summed = jnp.dot(weights.astype(jnp.bfloat16), cluster, preferred_element_type=jnp.float32)
    log_weight = row_top + jnp.log(totals)
    first = log_weight.astype(jnp.bfloat16).astype(jnp.float32)
    rest = log_weight - first
    second = rest.astype(jnp.bfloat16).astype(jnp.float32)
    third = rest - second
    lane = lax.broadcasted_iota(jnp.int32, (flat.shape[0], LANES), 1) % TERM_LANES
    terms = jnp.where(lane == 0, first, jnp.where(lane == 1, second, third))
    return summed * (1.0 / totals), terms


def score_kernel(*refs):
    part_refs, refs = refs[:DEPTH], refs[DEPTH:]
    cluster_refs, norm_refs, out_refs = refs[:CORES], refs[CORES : 2 * CORES], refs[2 * CORES :]
    size, rows, features = part_refs[0].shape
    half = size // CORES
    first_half = lax.broadcasted_iota(jnp.int32, (rows, LANES), 1) < LANES // 2
    for side in range(CORES):
        span = slice(side * half, (side + 1) * half)
        flat = jnp.concatenate(
            [
                part_ref[span].astype(jnp.float32).reshape(half * rows, features)
                for part_ref in part_refs
            ]
        ).astype(jnp.bfloat16)
        part, terms = score(flat, cluster_refs[side][...], norm_refs[side][...])
        for place, out_ref in enumerate(out_refs):
            first = place * half * rows
            lines = part[first : first + half * rows]
            out_ref[span] = lines.reshape(half, rows, features).astype(jnp.bfloat16)
            for index in range(0, half, 2):
                line = first + index * rows
                both = jnp.where(
                    first_half, terms[line : line + rows], terms[line + rows : line + 2 * rows]
                )
                lanes = (side * half + index) // 2 * LANES
                out_ref[size, :, lanes : lanes + LANES] = both.astype(jnp.bfloat16)


def score_parts(parts, clusters, norms):
    size, rows, features = parts[0].shape
    references = clusters[0].shape[0]
    total = DEPTH * size * rows
    out = jax.ShapeDtypeStruct((size + 1, rows, features), jnp.bfloat16)
    return pl.pallas_call(
        score_kernel,
        out_shape=[out] * DEPTH,
        in_specs=[VMEM] * (DEPTH + 2 * CORES),
        out_specs=[VMEM] * DEPTH,
        compiler_params=params(),
        cost_estimate=pl.CostEstimate(
            flops=4 * total * references * features,
            bytes_accessed=2 * (2 * total * features + CORES * references * features),
            transcendentals=total * references,
        ),
    )(*parts, *clusters, *norms)


def combine_kernel(log_count, slots_ref, blocks_ref, returned_ref, mixed_ref, density_ref, *send_refs):
    count, _, features = blocks_ref.shape
    tiles = features // LANES
    per_slab = 2 * count // SLABS
    lane = lax.broadcasted_iota(jnp.int32, density_ref.shape, 1)
    lane_slot = jnp.where(
        lane % TERM_LANES < TERMS, lane % (LANES // 2) // TERM_LANES, -1
    )

    def read(slot):
        base, last, rank = chunk_base(slot, per_slab, tiles)
        part = returned_ref[pl.ds(base, tiles)].astype(jnp.float32)
        terms = returned_ref[last].astype(jnp.float32)
        terms = jnp.where(lane_slot == rank, terms, 0.0)
        return part, jnp.sum(terms, axis=1, keepdims=True)

    def body(block, densities):
        first_slot, second_slot = slots_ref[2 * block], slots_ref[2 * block + 1]
        first_part, first_log = read(first_slot)
        second_part, second_log = read(second_slot)
        both_top = jnp.maximum(first_log, second_log)
        first_share = jnp.exp(first_log - both_top)
        second_share = jnp.exp(second_log - both_top)
        pair_total = first_share + second_share
        inverse = 1.0 / pair_total
        mixed = (
            (first_share * inverse)[None] * first_part
            + (second_share * inverse)[None] * second_part
        ).astype(jnp.bfloat16)
        squares = jnp.sum(
            jnp.square(blocks_ref[block].astype(jnp.float32)), axis=1, keepdims=True
        )
        density = both_top + jnp.log(pair_total) - 0.5 * INV_WIDTH * squares - log_count
        for tile in range(tiles):
            lanes = slice(tile * LANES, (tile + 1) * LANES)
            mixed_ref[block, :, lanes] = mixed[tile]
            for send_ref in send_refs:
                send_ref[first_slot, :, lanes] = mixed[tile]
                send_ref[second_slot, :, lanes] = mixed[tile]
        return jnp.where(lane == block, density, densities)

    density_ref[...] = lax.fori_loop(
        0, blocks_ref.shape[0], body, jnp.zeros(density_ref.shape, jnp.float32), unroll=4
    )


def combine(blocks, returned, slots, log_count, send):
    count, rows, features = blocks.shape
    outs = [
        jax.ShapeDtypeStruct(blocks.shape, jnp.bfloat16),
        jax.ShapeDtypeStruct((rows, LANES), jnp.float32),
    ]
    if send:
        outs.append(jax.ShapeDtypeStruct((2 * count, rows, features), jnp.bfloat16))
    return pl.pallas_call(
        functools.partial(combine_kernel, log_count),
        out_shape=outs,
        in_specs=[SMEM, VMEM, VMEM],
        out_specs=[VMEM] * len(outs),
        compiler_params=params(),
    )(slots, blocks, returned)


def half_norms_of(cluster_rows):
    return 0.5 * jnp.sum(jnp.square(cluster_rows.astype(jnp.float32)), axis=1)[None, :]


def sorted_origins(arrived, total, depth, core):
    chunks = arrived.reshape(SLABS, -1, *arrived.shape[1:])
    targets = chunks[:, -1, 0, : total // SLABS].reshape(-1).astype(jnp.int32)
    per_cluster = total // CLUSTER_DEVICES
    order = jnp.arange(total, dtype=jnp.int32)
    earlier = (targets[:, None] == targets[None, :]) & (order[None, :] < order[:, None])
    rank = jnp.sum(earlier.astype(jnp.int32), axis=1)
    shift = (targets // CORES - depth) % DEPTH
    place = shift ^ (shift >> 1)
    side = (targets % CORES) ^ core
    slot = (place * CORES + side) * per_cluster + rank
    return jnp.sum(jnp.where(slot[None, :] == order[:, None], order[None, :], 0), axis=1)


def local(queries, corpus, block_pairs, owner_table):
    features = queries.shape[2]
    cluster_index = lax.axis_index("cluster").astype(jnp.int32)
    depth, core = cluster_index // CORES, cluster_index % CORES
    own = corpus[0]
    log_count = math.log(2.0 * own.shape[0])
    current = queries
    outgoing, slots = fill(current, block_pairs.T, owner_table)
    origin = None
    densities = []
    for step in range(STEPS):
        arrived = exchange_slabs(outgoing)
        if step == 0:
            arrived, own = lax.optimization_barrier((arrived, own))
            other = swap_cores(own)
            clusters = (own, other)
            norms = (half_norms_of(own), half_norms_of(other))
            origin = sorted_origins(arrived, slots.shape[0], depth, core)
        parts = sort_by_depth(arrived, origin, features)
        parts = [parts[0]] + [shift_depth(p, k) for p, k in zip(parts[1:], SHIFTS[1:])]
        answers = score_parts(parts, clusters, norms)
        answers = [answers[0]] + [shift_depth(a, -k) for a, k in zip(answers[1:], SHIFTS[1:])]
        returned = exchange_slabs(unsort(answers, origin))
        current, density, *outgoing = combine(
            current, returned, slots, log_count, step < STEPS - 1
        )
        outgoing = outgoing[0] if outgoing else None
        densities.append(density[:, : queries.shape[0]])
    return (current, jnp.stack(densities).transpose(0, 2, 1).reshape(STEPS, -1))


def solution(mesh):
    return jax.shard_map(
        local,
        mesh=mesh,
        in_specs=(
            P(("cluster", "slab"), None, None),
            P(("cluster", "slab"), None, None),
            P(("cluster", "slab"), None),
            P(),
        ),
        out_specs=(P(("cluster", "slab"), None, None), P(None, ("cluster", "slab"))),
        check_vma=False,
    )
```

```python
import functools
import math

import jax
import jax.numpy as jnp
from jax import lax
from jax.experimental import pallas as pl
from jax.experimental.pallas import tpu as pltpu
from jax.sharding import PartitionSpec as P

STEPS = 2
INV_WIDTH = 1.0 / 16.0
LANES = 128
VMEM_LIMIT = 48 * 1024 * 1024
AXES = ("cluster", "slab")
SIDE = 4
CORES = 2
DEPTH = 4
SLABS = SIDE * SIDE
CLUSTER_DEVICES = DEPTH * CORES
OWN, OTHER, AHEAD, OTHER_AHEAD = range(4)
GROUPS = ((OWN, OTHER), (AHEAD, OTHER_AHEAD), (AHEAD, OTHER), (OWN, OTHER_AHEAD))
STAY = 2
HALVES = ((0, 2, 4, 6), (1, 5, 7, 3))
TERM_LANES = 8
TERMS = 3


def slab_order(core):
    order = [(a, (a + b) % SIDE) for b in range(SIDE) for a in range(SIDE)]
    return [x * SIDE + y if core == 0 else y * SIDE + x for x, y in order]


def slab_groups():
    return [
        [cluster * SLABS + slab for slab in slab_order(cluster % CORES)]
        for cluster in range(CLUSTER_DEVICES)
    ]


def exchange_slabs(array):
    return lax.all_to_all(
        array, AXES, split_axis=0, concat_axis=0, tiled=True, axis_index_groups=slab_groups()
    )


def send_ahead(array, steps):
    pairs = []
    for z in range(DEPTH):
        for core in range(CORES):
            target_z = (z + (steps if core == 0 else -steps)) % DEPTH
            for slab in range(SLABS):
                source = (z * CORES + core) * SLABS + slab
                target = (target_z * CORES + core) * SLABS + slab
                pairs.append((source, target))
    return lax.ppermute(array, AXES, pairs)


def swap_cores(array):
    pairs = []
    for cluster in range(CLUSTER_DEVICES):
        for slab in range(SLABS):
            pairs.append((cluster * SLABS + slab, (cluster ^ 1) * SLABS + slab))
    return lax.ppermute(array, AXES, pairs)


def whole(space):
    return pl.BlockSpec(memory_space=space)


SMEM, VMEM = whole(pltpu.SMEM), whole(pltpu.VMEM)


def params():
    return pltpu.CompilerParams(vmem_limit_bytes=VMEM_LIMIT)


def slab_place(slab, core):
    x, y = lax.div(slab, SIDE), lax.rem(slab, SIDE)
    first, second = jnp.where(core == 0, x, y), jnp.where(core == 0, y, x)
    return lax.rem(second - first + SIDE, SIDE) * SIDE + first


def fill_kernel(
    pairs_hbm, table_hbm, blocks_hbm, out_ref, slots_ref, squares_ref,
    pairs_ref, table_ref, blocks_ref, counts_ref, targets_ref, input_sems,
):
    count, rows, features = blocks_ref.shape
    tiles = features // LANES
    per_slab = 2 * count // SLABS
    core = lax.rem(lax.axis_index("cluster").astype(jnp.int32), CORES)
    inputs = [
        pltpu.make_async_copy(pairs_hbm, pairs_ref, input_sems.at[0]),
        pltpu.make_async_copy(table_hbm, table_ref, input_sems.at[1]),
        pltpu.make_async_copy(blocks_hbm, blocks_ref, input_sems.at[2]),
    ]
    for copy in inputs:
        copy.start()
    for place in range(SLABS):
        counts_ref[place] = 0
    for copy in inputs[:2]:
        copy.wait()

    def assign(block, carry):
        for side in range(2):
            entry = table_ref[pairs_ref[side, block]]
            place = slab_place(lax.rem(entry, SLABS), core)
            rank = counts_ref[place]
            counts_ref[place] = rank + 1
            slot = place * per_slab + rank
            slots_ref[2 * block + side] = slot
            targets_ref[slot] = lax.div(entry, SLABS)
        return carry

    lax.fori_loop(0, count, assign, 0, unroll=4)
    inputs[2].wait()
    lane = lax.broadcasted_iota(jnp.int32, (rows, LANES), 1)

    def put(block, squares):
        bases = [chunk_base(slots_ref[2 * block + side], per_slab, tiles)[0] for side in range(2)]
        total = jnp.zeros((rows, LANES), jnp.float32)
        for tile in range(tiles):
            values = blocks_ref[block, :, tile * LANES : (tile + 1) * LANES]
            for base in bases:
                out_ref[base + tile] = values
            total += jnp.square(values.astype(jnp.float32))
        return jnp.where(lane == block, jnp.sum(total, axis=1, keepdims=True), squares)

    squares_ref[...] = lax.fori_loop(
        0, count, put, jnp.zeros((rows, LANES), jnp.float32), unroll=4
    )

    def note(place, carry):
        tile = jnp.zeros((rows, LANES), jnp.int32)
        for rank in range(per_slab):
            tile = jnp.where(lane == rank, targets_ref[place * per_slab + rank], tile)
        tile = tile.astype(jnp.float32).astype(jnp.bfloat16)
        out_ref[place * (per_slab * tiles + 1) + per_slab * tiles] = tile
        return carry

    lax.fori_loop(0, SLABS, note, 0, unroll=4)


def fill(blocks, pairs, table):
    count, rows, features = blocks.shape
    chunk = 2 * count // SLABS * (features // LANES) + 1
    pairs = pltpu.with_memory_space_constraint(pairs, pltpu.HBM)
    table = pltpu.with_memory_space_constraint(table, pltpu.HBM)
    blocks = pltpu.with_memory_space_constraint(blocks, pltpu.HBM)
    hbm = whole(pltpu.HBM)
    return pl.pallas_call(
        fill_kernel,
        out_shape=[
            jax.ShapeDtypeStruct((SLABS * chunk, rows, LANES), jnp.bfloat16),
            jax.ShapeDtypeStruct((2 * count,), jnp.int32),
            jax.ShapeDtypeStruct((rows, LANES), jnp.float32),
        ],
        in_specs=[hbm, hbm, hbm],
        out_specs=[VMEM, SMEM, VMEM],
        scratch_shapes=[
            pltpu.SMEM(pairs.shape, jnp.int32),
            pltpu.SMEM(table.shape, jnp.int32),
            pltpu.VMEM(blocks.shape, jnp.bfloat16),
            pltpu.SMEM((SLABS,), jnp.int32),
            pltpu.SMEM((2 * count,), jnp.int32),
            pltpu.SemaphoreType.DMA((3,)),
        ],
        compiler_params=params(),
    )(pairs, table, blocks)


def chunk_base(message, per_slab, tiles):
    place, rank = lax.div(message, per_slab), lax.rem(message, per_slab)
    first = place * (per_slab * tiles + 1)
    return first + rank * tiles, first + per_slab * tiles, rank


def sort_kernel(origin_ref, arrived_ref, *out_refs):
    size, _, features = out_refs[0].shape
    tiles = features // LANES
    per_slab = len(GROUPS) * size // SLABS
    chunked = arrived_ref.shape[2] != features
    for place, out_ref in enumerate(out_refs):

        def body(index, carry, place=place, out_ref=out_ref):
            origin = origin_ref[place * size + index]
            if not chunked:
                out_ref[index] = arrived_ref[origin]
                return carry
            base, _, _ = chunk_base(origin, per_slab, tiles)
            for tile in range(tiles):
                out_ref[index, :, tile * LANES : (tile + 1) * LANES] = arrived_ref[base + tile]
            return carry

        lax.fori_loop(0, size, body, 0, unroll=4)


def sort_by_depth(arrived, origin, features):
    total, rows = origin.shape[0], arrived.shape[1]
    part = jax.ShapeDtypeStruct((total // len(GROUPS), rows, features), jnp.bfloat16)
    return pl.pallas_call(
        sort_kernel,
        out_shape=[part] * len(GROUPS),
        in_specs=[SMEM, VMEM],
        out_specs=[VMEM] * len(GROUPS),
        compiler_params=params(),
    )(origin, arrived)


def unsort_kernel(origin_ref, *refs):
    part_refs, out_ref, logs_ref = refs[:-2], refs[-2], refs[-1]
    size, rows, features = part_refs[0].shape
    size -= 1
    tiles = features // LANES
    total = len(GROUPS) * size
    per_slab = total // SLABS
    lane = lax.broadcasted_iota(jnp.int32, (rows, LANES), 1)
    halves = [lane < LANES // 2, lane >= LANES // 2]
    for place, part_ref in enumerate(part_refs):
        for index in range(size):
            origin = origin_ref[place * size + index]
            base, _, _ = chunk_base(origin, per_slab, tiles)
            for tile in range(tiles):
                out_ref[base + tile] = part_ref[index, :, tile * LANES : (tile + 1) * LANES]
            first = index // 2 * LANES
            terms = part_ref[size, :, first : first + LANES].astype(jnp.float32)
            logs_ref[origin] = jnp.where(halves[index % 2], terms, 0.0)
    slot = lane % (LANES // 2) // TERM_LANES

    def pack(place, carry):
        tile = logs_ref[place * per_slab]
        for rank in range(1, per_slab):
            tile = jnp.where(slot == rank, logs_ref[place * per_slab + rank], tile)
        out_ref[place * (per_slab * tiles + 1) + per_slab * tiles] = tile.astype(jnp.bfloat16)
        return carry

    lax.fori_loop(0, SLABS, pack, 0, unroll=4)


def unsort(parts, origin):
    size, rows, features = parts[0].shape
    total = origin.shape[0]
    chunk = total // SLABS * (features // LANES) + 1
    return pl.pallas_call(
        unsort_kernel,
        out_shape=jax.ShapeDtypeStruct((SLABS * chunk, rows, LANES), jnp.bfloat16),
        in_specs=[SMEM] + [VMEM] * len(GROUPS),
        out_specs=VMEM,
        scratch_shapes=[pltpu.VMEM((total, rows, LANES), jnp.float32)],
        compiler_params=params(),
    )(origin, *parts)


def products_of(flat, cluster):
    return lax.dot_general(
        flat, cluster, (((1,), (1,)), ((), ())), preferred_element_type=jnp.float32
    )


def weigh(products, norms):
    scores = (products - norms) * INV_WIDTH
    row_top = jnp.max(scores, axis=1, keepdims=True)
    weights = jnp.exp(scores - row_top)
    totals = jnp.sum(weights, axis=1, keepdims=True)
    log_weight = row_top + jnp.log(totals)
    first = log_weight.astype(jnp.bfloat16).astype(jnp.float32)
    rest = log_weight - first
    second = rest.astype(jnp.bfloat16).astype(jnp.float32)
    third = rest - second
    lane = lax.broadcasted_iota(jnp.int32, (products.shape[0], LANES), 1) % TERM_LANES
    terms = jnp.where(lane == 0, first, jnp.where(lane == 1, second, third))
    return weights.astype(jnp.bfloat16), totals, terms


def score_kernel(*refs):
    count = len(GROUPS)
    part_refs, refs = refs[:count], refs[count:]
    cluster_anys, refs = refs[:count], refs[count:]
    norm_refs, refs = refs[:count], refs[count:]
    out_refs, (clusters_ref, cluster_sems) = refs[:count], refs[count:]
    copies = [
        pltpu.make_async_copy(cluster_any, clusters_ref.at[index], cluster_sems.at[index])
        for index, cluster_any in enumerate(cluster_anys)
    ]
    for copy in copies:
        copy.start()
    size, rows, features = part_refs[0].shape
    half = size // 2
    lines = half * rows
    first_half = lax.broadcasted_iota(jnp.int32, (rows, LANES), 1) < LANES // 2
    members = [
        [(group, side) for group, pair in enumerate(GROUPS) for side in range(2) if pair[side] == cluster]
        for cluster in range(count)
    ]
    products = []
    for cluster in range(count):
        flat = jnp.concatenate(
            [
                part_refs[group][side * half : (side + 1) * half]
                .astype(jnp.float32)
                .reshape(lines, features)
                for group, side in members[cluster]
            ]
        ).astype(jnp.bfloat16)
        copies[cluster].wait()
        products.append(products_of(flat, clusters_ref[cluster]))
    for cluster in range(count):
        weights, totals, terms = weigh(products[cluster], norm_refs[cluster][...])
        summed = jnp.dot(weights, clusters_ref[cluster], preferred_element_type=jnp.float32)
        part = summed * (1.0 / totals)
        for place, (group, side) in enumerate(members[cluster]):
            first, out_ref = place * lines, out_refs[group]
            out_ref[side * half : (side + 1) * half] = (
                part[first : first + lines].reshape(half, rows, features).astype(jnp.bfloat16)
            )
            for index in range(0, half, 2):
                line = first + index * rows
                both = jnp.where(
                    first_half, terms[line : line + rows], terms[line + rows : line + 2 * rows]
                )
                lanes = (side * half + index) // 2 * LANES
                out_ref[size, :, lanes : lanes + LANES] = both.astype(jnp.bfloat16)


def score_parts(parts, clusters, norms):
    count = len(GROUPS)
    size, rows, features = parts[0].shape
    references = clusters[0].shape[0]
    total = count * size * rows
    out = jax.ShapeDtypeStruct((size + 1, rows, features), jnp.bfloat16)
    return pl.pallas_call(
        score_kernel,
        out_shape=[out] * count,
        in_specs=[VMEM] * count + [whole(pl.ANY)] * count + [VMEM] * count,
        out_specs=[VMEM] * count,
        scratch_shapes=[
            pltpu.VMEM((count, references, features), jnp.bfloat16),
            pltpu.SemaphoreType.DMA((count,)),
        ],
        compiler_params=params(),
        cost_estimate=pl.CostEstimate(
            flops=4 * total * references * features,
            bytes_accessed=2 * (2 * total * features + count * references * features),
            transcendentals=total * references,
        ),
    )(*parts, *clusters, *norms)


def combine_kernel(log_count, step, slots_ref, squares_ref, returned_ref, earlier_ref, *out_refs):
    density_ref, *out_refs = out_refs
    rows = squares_ref.shape[0]
    count = slots_ref.shape[0] // 2
    per_slab = 2 * count // SLABS
    tiles = (returned_ref.shape[0] // SLABS - 1) // per_slab
    row = lax.broadcasted_iota(jnp.int32, (rows, LANES), 0)
    lane = lax.broadcasted_iota(jnp.int32, (rows, LANES), 1)
    lane_slot = jnp.where(
        lane % TERM_LANES < TERMS, lane % (LANES // 2) // TERM_LANES, -1
    )
    last = len(out_refs) == 1
    squares = squares_ref[...]

    def read(slot):
        base, shared, rank = chunk_base(slot, per_slab, tiles)
        part = returned_ref[pl.ds(base, tiles)].astype(jnp.float32)
        terms = returned_ref[shared].astype(jnp.float32)
        terms = jnp.where(lane_slot == rank, terms, 0.0)
        return part, jnp.sum(terms, axis=1, keepdims=True)

    def body(block, carry):
        densities, next_squares = carry
        first_slot, second_slot = slots_ref[2 * block], slots_ref[2 * block + 1]
        first_part, first_log = read(first_slot)
        second_part, second_log = read(second_slot)
        both_top = jnp.maximum(first_log, second_log)
        first_share = jnp.exp(first_log - both_top)
        second_share = jnp.exp(second_log - both_top)
        pair_total = first_share + second_share
        inverse = 1.0 / pair_total
        mixed = (
            (first_share * inverse)[None] * first_part
            + (second_share * inverse)[None] * second_part
        ).astype(jnp.bfloat16)
        density = both_top + jnp.log(pair_total)
        densities = jnp.where(lane == block, density, densities)
        if last:
            for tile in range(tiles):
                out_refs[0][block, :, tile * LANES : (tile + 1) * LANES] = mixed[tile]
            return densities, next_squares
        for tile in range(tiles):
            lanes = slice(tile * LANES, (tile + 1) * LANES)
            out_refs[0][first_slot, :, lanes] = mixed[tile]
            out_refs[0][second_slot, :, lanes] = mixed[tile]
        total = jnp.sum(jnp.square(mixed.astype(jnp.float32)), axis=0)
        total = jnp.sum(total, axis=1, keepdims=True)
        return densities, jnp.where(lane == block, total, next_squares)

    zeros = jnp.zeros((rows, LANES), jnp.float32)
    densities, next_squares = lax.fori_loop(0, count, body, (zeros, zeros), unroll=4)
    if not last:
        out_refs[1][...] = next_squares
    densities = densities - 0.5 * INV_WIDTH * squares - log_count
    blocks_wide = LANES // rows
    for wide in range(count // blocks_wide):
        spread = zeros
        for index in range(blocks_wide):
            block = wide * blocks_wide + index
            column = densities[:, block : block + 1]
            spread = jnp.where(lane == index * rows + row, column, spread)
        line = jnp.sum(
            jnp.where(lane % rows == row, spread, 0.0), axis=0, keepdims=True
        )
        lanes = slice(wide * LANES, (wide + 1) * LANES)
        for other in range(density_ref.shape[0]):
            if other == step:
                density_ref[other : other + 1, lanes] = line
            else:
                density_ref[other : other + 1, lanes] = earlier_ref[other : other + 1, lanes]


def combine(squares, returned, slots, earlier, log_count, step, features):
    rows = squares.shape[0]
    total = slots.shape[0]
    outs = [jax.ShapeDtypeStruct(earlier.shape, jnp.float32)]
    if step == STEPS - 1:
        outs.append(jax.ShapeDtypeStruct((total // 2, rows, features), jnp.bfloat16))
    else:
        outs.append(jax.ShapeDtypeStruct((total, rows, features), jnp.bfloat16))
        outs.append(jax.ShapeDtypeStruct(squares.shape, jnp.float32))
    return pl.pallas_call(
        functools.partial(combine_kernel, log_count, step),
        out_shape=outs,
        in_specs=[SMEM, VMEM, VMEM, VMEM],
        out_specs=[VMEM] * len(outs),
        compiler_params=params(),
    )(slots, squares, returned, earlier)


def half_norms_of(cluster_rows):
    return 0.5 * jnp.sum(jnp.square(cluster_rows.astype(jnp.float32)), axis=1)[None, :]


def sorted_origins(arrived, total, depth, core):
    chunks = arrived.reshape(SLABS, -1, *arrived.shape[1:])
    targets = chunks[:, -1, 0, : total // SLABS].reshape(-1).astype(jnp.int32)
    order = jnp.arange(total, dtype=jnp.int32)
    earlier = (targets[:, None] == targets[None, :]) & (order[None, :] < order[:, None])
    rank = jnp.sum(earlier.astype(jnp.int32), axis=1)
    side = (targets % CORES) ^ core
    ahead = targets // CORES - depth
    ahead = jnp.where(core == 0, ahead, -ahead) % DEPTH
    half = sum(
        jnp.where((side == at) & (ahead == steps), HALVES[at][steps], 0)
        for at in range(CORES)
        for steps in range(DEPTH)
    )
    slot = half * (total // CLUSTER_DEVICES) + rank
    return jnp.sum(jnp.where(slot[None, :] == order[:, None], order[None, :], 0), axis=1)


def local(queries, corpus, block_pairs, owner_table):
    features = queries.shape[2]
    cluster_index = lax.axis_index("cluster").astype(jnp.int32)
    depth, core = cluster_index // CORES, cluster_index % CORES
    own = corpus[0]
    ahead = send_ahead(own, -1)
    other = swap_cores(own)
    log_count = math.log(2.0 * own.shape[0])
    outgoing, slots, squares = fill(queries, block_pairs.T, owner_table)
    densities = jnp.zeros((STEPS, queries.shape[0] * queries.shape[1]), jnp.float32)
    for step in range(STEPS):
        arrived = exchange_slabs(outgoing)
        if step == 0:
            ahead, arrived = lax.optimization_barrier((ahead, arrived))
            clusters = (own, other, ahead, swap_cores(ahead))
            norms = [half_norms_of(cluster) for cluster in clusters]
            origin = sorted_origins(arrived, slots.shape[0], depth, core)
        parts = list(sort_by_depth(arrived, origin, features))
        parts[STAY:] = [send_ahead(parts[STAY], 1), send_ahead(parts[STAY + 1], -1)]
        answers = list(score_parts(parts, clusters, norms))
        answers[STAY:] = [send_ahead(answers[STAY], -1), send_ahead(answers[STAY + 1], 1)]
        returned = exchange_slabs(unsort(answers, origin))
        densities, outgoing, *squares_next = combine(
            squares, returned, slots, densities, log_count, step, features
        )
        squares = squares_next[0] if squares_next else None
    return (outgoing, densities)


def solution(mesh):
    return jax.shard_map(
        local,
        mesh=mesh,
        in_specs=(
            P(("cluster", "slab"), None, None),
            P(("cluster", "slab"), None, None),
            P(("cluster", "slab"), None),
            P(),
        ),
        out_specs=(P(("cluster", "slab"), None, None), P(None, ("cluster", "slab"))),
        check_vma=False,
    )
```

```python
import functools
import math

import jax
import jax.numpy as jnp
from jax import lax
from jax.experimental import pallas as pl
from jax.experimental.pallas import tpu as pltpu
from jax.sharding import PartitionSpec as P

STEPS = 2
INV_WIDTH = 1.0 / 16.0
LANES = 128
VMEM_LIMIT = 48 * 1024 * 1024
AXES = ("cluster", "slab")
SIDE = 4
CORES = 2
DEPTH = 4
SLABS = SIDE * SIDE
CLUSTER_DEVICES = DEPTH * CORES
OWN, OTHER, AHEAD, OTHER_AHEAD = range(4)
GROUPS = ((OWN, OTHER), (AHEAD, OTHER_AHEAD), (AHEAD, OTHER), (OWN, OTHER_AHEAD))
STAY = 2
HALVES = ((0, 2, 4, 6), (1, 5, 7, 3))
TERM_LANES = 8
TERMS = 3


def slab_order(core):
    order = [(a, (a + b) % SIDE) for b in range(SIDE) for a in range(SIDE)]
    return [x * SIDE + y if core == 0 else y * SIDE + x for x, y in order]


def slab_groups():
    return [
        [cluster * SLABS + slab for slab in slab_order(cluster % CORES)]
        for cluster in range(CLUSTER_DEVICES)
    ]


def exchange_slabs(array):
    return lax.all_to_all(
        array, AXES, split_axis=0, concat_axis=0, tiled=True, axis_index_groups=slab_groups()
    )


def send_ahead(array, steps):
    pairs = []
    for z in range(DEPTH):
        for core in range(CORES):
            target_z = (z + (steps if core == 0 else -steps)) % DEPTH
            for slab in range(SLABS):
                source = (z * CORES + core) * SLABS + slab
                target = (target_z * CORES + core) * SLABS + slab
                pairs.append((source, target))
    return lax.ppermute(array, AXES, pairs)


def swap_cores(array):
    pairs = []
    for cluster in range(CLUSTER_DEVICES):
        for slab in range(SLABS):
            pairs.append((cluster * SLABS + slab, (cluster ^ 1) * SLABS + slab))
    return lax.ppermute(array, AXES, pairs)


def whole(space):
    return pl.BlockSpec(memory_space=space)


SMEM, VMEM = whole(pltpu.SMEM), whole(pltpu.VMEM)


def params():
    return pltpu.CompilerParams(vmem_limit_bytes=VMEM_LIMIT)


def slab_place(slab, core):
    x, y = lax.div(slab, SIDE), lax.rem(slab, SIDE)
    first, second = jnp.where(core == 0, x, y), jnp.where(core == 0, y, x)
    return lax.rem(second - first + SIDE, SIDE) * SIDE + first


def fill_kernel(
    pairs_hbm, table_hbm, blocks_hbm, out_ref, slots_ref, squares_ref,
    pairs_ref, table_ref, blocks_ref, counts_ref, targets_ref, input_sems,
):
    count, rows, features = blocks_ref.shape
    tiles = features // LANES
    per_slab = 2 * count // SLABS
    core = lax.rem(lax.axis_index("cluster").astype(jnp.int32), CORES)
    inputs = [
        pltpu.make_async_copy(pairs_hbm, pairs_ref, input_sems.at[0]),
        pltpu.make_async_copy(table_hbm, table_ref, input_sems.at[1]),
        pltpu.make_async_copy(blocks_hbm, blocks_ref, input_sems.at[2]),
    ]
    for copy in inputs:
        copy.start()
    for place in range(SLABS):
        counts_ref[place] = 0
    for copy in inputs[:2]:
        copy.wait()

    def assign(block, carry):
        for side in range(2):
            entry = table_ref[pairs_ref[side, block]]
            place = slab_place(lax.rem(entry, SLABS), core)
            rank = counts_ref[place]
            counts_ref[place] = rank + 1
            slot = place * per_slab + rank
            slots_ref[2 * block + side] = slot
            targets_ref[slot] = lax.div(entry, SLABS)
        return carry

    lax.fori_loop(0, count, assign, 0, unroll=8)
    inputs[2].wait()
    lane = lax.broadcasted_iota(jnp.int32, (rows, LANES), 1)

    def put(block, squares):
        bases = [chunk_base(slots_ref[2 * block + side], per_slab, tiles)[0] for side in range(2)]
        total = jnp.zeros((rows, LANES), jnp.float32)
        for tile in range(tiles):
            values = blocks_ref[block, :, tile * LANES : (tile + 1) * LANES]
            for base in bases:
                out_ref[base + tile] = values
            total += jnp.square(values.astype(jnp.float32))
        return jnp.where(lane == block, jnp.sum(total, axis=1, keepdims=True), squares)

    squares_ref[...] = lax.fori_loop(
        0, count, put, jnp.zeros((rows, LANES), jnp.float32), unroll=8
    )

    def note(place, carry):
        tile = jnp.zeros((rows, LANES), jnp.int32)
        for rank in range(per_slab):
            tile = jnp.where(lane == rank, targets_ref[place * per_slab + rank], tile)
        tile = tile.astype(jnp.float32).astype(jnp.bfloat16)
        out_ref[place * (per_slab * tiles + 1) + per_slab * tiles] = tile
        return carry

    lax.fori_loop(0, SLABS, note, 0, unroll=16)


def fill(blocks, pairs, table):
    count, rows, features = blocks.shape
    chunk = 2 * count // SLABS * (features // LANES) + 1
    pairs = pltpu.with_memory_space_constraint(pairs, pltpu.HBM)
    table = pltpu.with_memory_space_constraint(table, pltpu.HBM)
    blocks = pltpu.with_memory_space_constraint(blocks, pltpu.HBM)
    hbm = whole(pltpu.HBM)
    return pl.pallas_call(
        fill_kernel,
        out_shape=[
            jax.ShapeDtypeStruct((SLABS * chunk, rows, LANES), jnp.bfloat16),
            jax.ShapeDtypeStruct((2 * count,), jnp.int32),
            jax.ShapeDtypeStruct((rows, LANES), jnp.float32),
        ],
        in_specs=[hbm, hbm, hbm],
        out_specs=[VMEM, SMEM, VMEM],
        scratch_shapes=[
            pltpu.SMEM(pairs.shape, jnp.int32),
            pltpu.SMEM(table.shape, jnp.int32),
            pltpu.VMEM(blocks.shape, jnp.bfloat16),
            pltpu.SMEM((SLABS,), jnp.int32),
            pltpu.SMEM((2 * count,), jnp.int32),
            pltpu.SemaphoreType.DMA((3,)),
        ],
        compiler_params=params(),
    )(pairs, table, blocks)


def chunk_base(message, per_slab, tiles):
    place, rank = lax.div(message, per_slab), lax.rem(message, per_slab)
    first = place * (per_slab * tiles + 1)
    return first + rank * tiles, first + per_slab * tiles, rank


def sort_kernel(origin_ref, arrived_ref, *out_refs):
    size, _, features = out_refs[0].shape
    tiles = features // LANES
    per_slab = len(GROUPS) * size // SLABS
    chunked = arrived_ref.shape[2] != features
    for place, out_ref in enumerate(out_refs):

        def body(index, carry, place=place, out_ref=out_ref):
            origin = origin_ref[place * size + index]
            if not chunked:
                out_ref[index] = arrived_ref[origin]
                return carry
            base, _, _ = chunk_base(origin, per_slab, tiles)
            for tile in range(tiles):
                out_ref[index, :, tile * LANES : (tile + 1) * LANES] = arrived_ref[base + tile]
            return carry

        lax.fori_loop(0, size, body, 0, unroll=16)


def sort_by_depth(arrived, origin, features):
    total, rows = origin.shape[0], arrived.shape[1]
    part = jax.ShapeDtypeStruct((total // len(GROUPS), rows, features), jnp.bfloat16)
    return pl.pallas_call(
        sort_kernel,
        out_shape=[part] * len(GROUPS),
        in_specs=[SMEM, VMEM],
        out_specs=[VMEM] * len(GROUPS),
        compiler_params=params(),
    )(origin, arrived)


def unsort_kernel(origin_ref, *refs):
    part_refs, out_ref, logs_ref = refs[:-2], refs[-2], refs[-1]
    size, rows, features = part_refs[0].shape
    size -= 1
    tiles = features // LANES
    total = len(GROUPS) * size
    per_slab = total // SLABS
    lane = lax.broadcasted_iota(jnp.int32, (rows, LANES), 1)
    halves = [lane < LANES // 2, lane >= LANES // 2]
    for place, part_ref in enumerate(part_refs):
        for index in range(size):
            origin = origin_ref[place * size + index]
            base, _, _ = chunk_base(origin, per_slab, tiles)
            for tile in range(tiles):
                out_ref[base + tile] = part_ref[index, :, tile * LANES : (tile + 1) * LANES]
            first = index // 2 * LANES
            terms = part_ref[size, :, first : first + LANES].astype(jnp.float32)
            logs_ref[origin] = jnp.where(halves[index % 2], terms, 0.0)
    slot = lane % (LANES // 2) // TERM_LANES

    def pack(place, carry):
        tile = logs_ref[place * per_slab]
        for rank in range(1, per_slab):
            tile = jnp.where(slot == rank, logs_ref[place * per_slab + rank], tile)
        out_ref[place * (per_slab * tiles + 1) + per_slab * tiles] = tile.astype(jnp.bfloat16)
        return carry

    lax.fori_loop(0, SLABS, pack, 0, unroll=16)


def unsort(parts, origin):
    size, rows, features = parts[0].shape
    total = origin.shape[0]
    chunk = total // SLABS * (features // LANES) + 1
    return pl.pallas_call(
        unsort_kernel,
        out_shape=jax.ShapeDtypeStruct((SLABS * chunk, rows, LANES), jnp.bfloat16),
        in_specs=[SMEM] + [VMEM] * len(GROUPS),
        out_specs=VMEM,
        scratch_shapes=[pltpu.VMEM((total, rows, LANES), jnp.float32)],
        compiler_params=params(),
    )(origin, *parts)


def products_of(flat, cluster):
    return lax.dot_general(
        flat, cluster, (((1,), (1,)), ((), ())), preferred_element_type=jnp.float32
    )


def weigh(products, norms):
    scores = (products - norms) * INV_WIDTH
    row_top = jnp.max(scores, axis=1, keepdims=True)
    weights = jnp.exp(scores - row_top)
    totals = jnp.sum(weights, axis=1, keepdims=True)
    log_weight = row_top + jnp.log(totals)
    first = log_weight.astype(jnp.bfloat16).astype(jnp.float32)
    rest = log_weight - first
    second = rest.astype(jnp.bfloat16).astype(jnp.float32)
    third = rest - second
    lane = lax.broadcasted_iota(jnp.int32, (products.shape[0], LANES), 1) % TERM_LANES
    terms = jnp.where(lane == 0, first, jnp.where(lane == 1, second, third))
    return weights.astype(jnp.bfloat16), totals, terms


def score_kernel(*refs):
    count = len(GROUPS)
    part_refs, refs = refs[:count], refs[count:]
    cluster_anys, refs = refs[:count], refs[count:]
    norm_refs, refs = refs[:count], refs[count:]
    out_refs, (clusters_ref, cluster_sems) = refs[:count], refs[count:]
    copies = [
        pltpu.make_async_copy(cluster_any, clusters_ref.at[index], cluster_sems.at[index])
        for index, cluster_any in enumerate(cluster_anys)
    ]
    for copy in copies:
        copy.start()
    size, rows, features = part_refs[0].shape
    half = size // 2
    lines = half * rows
    first_half = lax.broadcasted_iota(jnp.int32, (rows, LANES), 1) < LANES // 2
    members = [
        [(group, side) for group, pair in enumerate(GROUPS) for side in range(2) if pair[side] == cluster]
        for cluster in range(count)
    ]
    products = []
    for cluster in range(count):
        flat = jnp.concatenate(
            [
                part_refs[group][side * half : (side + 1) * half]
                .astype(jnp.float32)
                .reshape(lines, features)
                for group, side in members[cluster]
            ]
        ).astype(jnp.bfloat16)
        copies[cluster].wait()
        products.append(products_of(flat, clusters_ref[cluster]))
    for cluster in range(count):
        weights, totals, terms = weigh(products[cluster], norm_refs[cluster][...])
        summed = jnp.dot(weights, clusters_ref[cluster], preferred_element_type=jnp.float32)
        part = summed * (1.0 / totals)
        for place, (group, side) in enumerate(members[cluster]):
            first, out_ref = place * lines, out_refs[group]
            out_ref[side * half : (side + 1) * half] = (
                part[first : first + lines].reshape(half, rows, features).astype(jnp.bfloat16)
            )
            for index in range(0, half, 2):
                line = first + index * rows
                both = jnp.where(
                    first_half, terms[line : line + rows], terms[line + rows : line + 2 * rows]
                )
                lanes = (side * half + index) // 2 * LANES
                out_ref[size, :, lanes : lanes + LANES] = both.astype(jnp.bfloat16)


def score_parts(parts, clusters, norms):
    count = len(GROUPS)
    size, rows, features = parts[0].shape
    references = clusters[0].shape[0]
    total = count * size * rows
    out = jax.ShapeDtypeStruct((size + 1, rows, features), jnp.bfloat16)
    return pl.pallas_call(
        score_kernel,
        out_shape=[out] * count,
        in_specs=[VMEM] * count + [whole(pl.ANY)] * count + [VMEM] * count,
        out_specs=[VMEM] * count,
        scratch_shapes=[
            pltpu.VMEM((count, references, features), jnp.bfloat16),
            pltpu.SemaphoreType.DMA((count,)),
        ],
        compiler_params=params(),
        cost_estimate=pl.CostEstimate(
            flops=4 * total * references * features,
            bytes_accessed=2 * (2 * total * features + count * references * features),
            transcendentals=total * references,
        ),
    )(*parts, *clusters, *norms)


def combine_kernel(log_count, step, slots_ref, squares_ref, returned_ref, earlier_ref, *out_refs):
    density_ref, *out_refs = out_refs
    rows = squares_ref.shape[0]
    count = slots_ref.shape[0] // 2
    per_slab = 2 * count // SLABS
    tiles = (returned_ref.shape[0] // SLABS - 1) // per_slab
    row = lax.broadcasted_iota(jnp.int32, (rows, LANES), 0)
    lane = lax.broadcasted_iota(jnp.int32, (rows, LANES), 1)
    lane_slot = jnp.where(
        lane % TERM_LANES < TERMS, lane % (LANES // 2) // TERM_LANES, -1
    )
    last = len(out_refs) == 1
    squares = squares_ref[...]

    def read(slot):
        base, shared, rank = chunk_base(slot, per_slab, tiles)
        part = returned_ref[pl.ds(base, tiles)].astype(jnp.float32)
        terms = returned_ref[shared].astype(jnp.float32)
        terms = jnp.where(lane_slot == rank, terms, 0.0)
        return part, jnp.sum(terms, axis=1, keepdims=True)

    def body(block, carry):
        densities, next_squares = carry
        first_slot, second_slot = slots_ref[2 * block], slots_ref[2 * block + 1]
        first_part, first_log = read(first_slot)
        second_part, second_log = read(second_slot)
        both_top = jnp.maximum(first_log, second_log)
        first_share = jnp.exp(first_log - both_top)
        second_share = jnp.exp(second_log - both_top)
        pair_total = first_share + second_share
        inverse = 1.0 / pair_total
        mixed = (
            (first_share * inverse)[None] * first_part
            + (second_share * inverse)[None] * second_part
        ).astype(jnp.bfloat16)
        density = both_top + jnp.log(pair_total)
        densities = jnp.where(lane == block, density, densities)
        if last:
            for tile in range(tiles):
                out_refs[0][block, :, tile * LANES : (tile + 1) * LANES] = mixed[tile]
            return densities, next_squares
        for tile in range(tiles):
            lanes = slice(tile * LANES, (tile + 1) * LANES)
            out_refs[0][first_slot, :, lanes] = mixed[tile]
            out_refs[0][second_slot, :, lanes] = mixed[tile]
        total = jnp.sum(jnp.square(mixed.astype(jnp.float32)), axis=0)
        total = jnp.sum(total, axis=1, keepdims=True)
        return densities, jnp.where(lane == block, total, next_squares)

    zeros = jnp.zeros((rows, LANES), jnp.float32)
    densities, next_squares = lax.fori_loop(0, count, body, (zeros, zeros), unroll=16)
    if not last:
        out_refs[1][...] = next_squares
    densities = densities - 0.5 * INV_WIDTH * squares - log_count
    blocks_wide = LANES // rows
    for wide in range(count // blocks_wide):
        spread = zeros
        for index in range(blocks_wide):
            block = wide * blocks_wide + index
            column = densities[:, block : block + 1]
            spread = jnp.where(lane == index * rows + row, column, spread)
        line = jnp.sum(
            jnp.where(lane % rows == row, spread, 0.0), axis=0, keepdims=True
        )
        lanes = slice(wide * LANES, (wide + 1) * LANES)
        for other in range(density_ref.shape[0]):
            if other == step:
                density_ref[other : other + 1, lanes] = line
            else:
                density_ref[other : other + 1, lanes] = earlier_ref[other : other + 1, lanes]


def combine(squares, returned, slots, earlier, log_count, step, features):
    rows = squares.shape[0]
    total = slots.shape[0]
    outs = [jax.ShapeDtypeStruct(earlier.shape, jnp.float32)]
    if step == STEPS - 1:
        outs.append(jax.ShapeDtypeStruct((total // 2, rows, features), jnp.bfloat16))
    else:
        outs.append(jax.ShapeDtypeStruct((total, rows, features), jnp.bfloat16))
        outs.append(jax.ShapeDtypeStruct(squares.shape, jnp.float32))
    return pl.pallas_call(
        functools.partial(combine_kernel, log_count, step),
        out_shape=outs,
        in_specs=[SMEM, VMEM, VMEM, VMEM],
        out_specs=[VMEM] * len(outs),
        compiler_params=params(),
    )(slots, squares, returned, earlier)


def half_norms_of(cluster_rows):
    return 0.5 * jnp.sum(jnp.square(cluster_rows.astype(jnp.float32)), axis=1)[None, :]


def sorted_origins(arrived, total, depth, core):
    chunks = arrived.reshape(SLABS, -1, *arrived.shape[1:])
    targets = chunks[:, -1, 0, : total // SLABS].reshape(-1).astype(jnp.int32)
    order = jnp.arange(total, dtype=jnp.int32)
    earlier = (targets[:, None] == targets[None, :]) & (order[None, :] < order[:, None])
    rank = jnp.sum(earlier.astype(jnp.int32), axis=1)
    side = (targets % CORES) ^ core
    ahead = targets // CORES - depth
    ahead = jnp.where(core == 0, ahead, -ahead) % DEPTH
    half = sum(
        jnp.where((side == at) & (ahead == steps), HALVES[at][steps], 0)
        for at in range(CORES)
        for steps in range(DEPTH)
    )
    slot = half * (total // CLUSTER_DEVICES) + rank
    return jnp.sum(jnp.where(slot[None, :] == order[:, None], order[None, :], 0), axis=1)


def local(queries, corpus, block_pairs, owner_table):
    features = queries.shape[2]
    cluster_index = lax.axis_index("cluster").astype(jnp.int32)
    depth, core = cluster_index // CORES, cluster_index % CORES
    own = corpus[0]
    ahead = send_ahead(own, -1)
    other = swap_cores(own)
    log_count = math.log(2.0 * own.shape[0])
    outgoing, slots, squares = fill(queries, block_pairs.T, owner_table)
    densities = jnp.zeros((STEPS, queries.shape[0] * queries.shape[1]), jnp.float32)
    for step in range(STEPS):
        arrived = exchange_slabs(outgoing)
        if step == 0:
            ahead, arrived = lax.optimization_barrier((ahead, arrived))
            clusters = (own, other, ahead, swap_cores(ahead))
            norms = [half_norms_of(cluster) for cluster in clusters]
            origin = sorted_origins(arrived, slots.shape[0], depth, core)
        parts = list(sort_by_depth(arrived, origin, features))
        parts[STAY:] = [send_ahead(parts[STAY], 1), send_ahead(parts[STAY + 1], -1)]
        answers = list(score_parts(parts, clusters, norms))
        answers[STAY:] = [send_ahead(answers[STAY], -1), send_ahead(answers[STAY + 1], 1)]
        returned = exchange_slabs(unsort(answers, origin))
        densities, outgoing, *squares_next = combine(
            squares, returned, slots, densities, log_count, step, features
        )
        squares = squares_next[0] if squares_next else None
    return (outgoing, densities)


def solution(mesh):
    return jax.shard_map(
        local,
        mesh=mesh,
        in_specs=(
            P(("cluster", "slab"), None, None),
            P(("cluster", "slab"), None, None),
            P(("cluster", "slab"), None),
            P(),
        ),
        out_specs=(P(("cluster", "slab"), None, None), P(None, ("cluster", "slab"))),
        check_vma=False,
    )
```

```python
import functools
import math

import jax
import jax.numpy as jnp
from jax import lax
from jax.experimental import pallas as pl
from jax.experimental.pallas import tpu as pltpu
from jax.sharding import PartitionSpec as P

STEPS = 2
INV_WIDTH = 1.0 / 16.0
LANES = 128
VMEM_LIMIT = 48 * 1024 * 1024
AXES = ("cluster", "slab")
SIDE = 4
CORES = 2
DEPTH = 4
SLABS = SIDE * SIDE
CLUSTER_DEVICES = DEPTH * CORES
OWN, OTHER, AHEAD, OTHER_AHEAD = range(4)
GROUPS = ((OWN, OTHER), (AHEAD, OTHER_AHEAD), (AHEAD, OTHER), (OWN, OTHER_AHEAD))
STAY = 2
HALVES = ((0, 2, 4, 6), (1, 5, 7, 3))
TERM_LANES = 8
TERMS = 3


def slab_order(core):
    order = [(a, (a + b) % SIDE) for b in range(SIDE) for a in range(SIDE)]
    return [x * SIDE + y if core == 0 else y * SIDE + x for x, y in order]


def slab_groups():
    return [
        [cluster * SLABS + slab for slab in slab_order(cluster % CORES)]
        for cluster in range(CLUSTER_DEVICES)
    ]


def exchange_slabs(array):
    return lax.all_to_all(
        array, AXES, split_axis=0, concat_axis=0, tiled=True, axis_index_groups=slab_groups()
    )


def send_ahead(array, steps):
    pairs = []
    for z in range(DEPTH):
        for core in range(CORES):
            target_z = (z + (steps if core == 0 else -steps)) % DEPTH
            for slab in range(SLABS):
                source = (z * CORES + core) * SLABS + slab
                target = (target_z * CORES + core) * SLABS + slab
                pairs.append((source, target))
    return lax.ppermute(array, AXES, pairs)


def swap_cores(array):
    pairs = []
    for cluster in range(CLUSTER_DEVICES):
        for slab in range(SLABS):
            pairs.append((cluster * SLABS + slab, (cluster ^ 1) * SLABS + slab))
    return lax.ppermute(array, AXES, pairs)


def whole(space):
    return pl.BlockSpec(memory_space=space)


SMEM, VMEM = whole(pltpu.SMEM), whole(pltpu.VMEM)


def params():
    return pltpu.CompilerParams(vmem_limit_bytes=VMEM_LIMIT)


def slab_place(slab, core):
    x, y = lax.div(slab, SIDE), lax.rem(slab, SIDE)
    first, second = jnp.where(core == 0, x, y), jnp.where(core == 0, y, x)
    return lax.rem(second - first + SIDE, SIDE) * SIDE + first


def fill_kernel(
    pairs_hbm, table_hbm, blocks_hbm, out_ref, slots_ref, squares_ref,
    pairs_ref, table_ref, blocks_ref, counts_ref, targets_ref, input_sems,
):
    count, rows, features = blocks_ref.shape
    tiles = features // LANES
    per_slab = 2 * count // SLABS
    core = lax.rem(lax.axis_index("cluster").astype(jnp.int32), CORES)
    inputs = [
        pltpu.make_async_copy(pairs_hbm, pairs_ref, input_sems.at[0]),
        pltpu.make_async_copy(table_hbm, table_ref, input_sems.at[1]),
        pltpu.make_async_copy(blocks_hbm, blocks_ref, input_sems.at[2]),
    ]
    for copy in inputs:
        copy.start()
    for place in range(SLABS):
        counts_ref[place] = 0
    for copy in inputs[:2]:
        copy.wait()

    def assign(block, carry):
        for side in range(2):
            entry = table_ref[pairs_ref[side, block]]
            place = slab_place(lax.rem(entry, SLABS), core)
            rank = counts_ref[place]
            counts_ref[place] = rank + 1
            slot = place * per_slab + rank
            slots_ref[2 * block + side] = slot
            targets_ref[slot] = lax.div(entry, SLABS)
        return carry

    lax.fori_loop(0, count, assign, 0, unroll=8)
    inputs[2].wait()
    lane = lax.broadcasted_iota(jnp.int32, (rows, LANES), 1)

    def put(block, squares):
        bases = [chunk_base(slots_ref[2 * block + side], per_slab, tiles)[0] for side in range(2)]
        total = jnp.zeros((rows, LANES), jnp.float32)
        for tile in range(tiles):
            values = blocks_ref[block, :, tile * LANES : (tile + 1) * LANES]
            for base in bases:
                out_ref[base + tile] = values
            total += jnp.square(values.astype(jnp.float32))
        return jnp.where(lane == block, jnp.sum(total, axis=1, keepdims=True), squares)

    squares_ref[...] = lax.fori_loop(
        0, count, put, jnp.zeros((rows, LANES), jnp.float32), unroll=8
    )

    def note(place, carry):
        tile = jnp.zeros((rows, LANES), jnp.int32)
        for rank in range(per_slab):
            tile = jnp.where(lane == rank, targets_ref[place * per_slab + rank], tile)
        tile = tile.astype(jnp.float32).astype(jnp.bfloat16)
        out_ref[place * (per_slab * tiles + 1) + per_slab * tiles] = tile
        return carry

    lax.fori_loop(0, SLABS, note, 0, unroll=16)


def fill(blocks, pairs, table):
    count, rows, features = blocks.shape
    chunk = 2 * count // SLABS * (features // LANES) + 1
    pairs = pltpu.with_memory_space_constraint(pairs, pltpu.HBM)
    table = pltpu.with_memory_space_constraint(table, pltpu.HBM)
    blocks = pltpu.with_memory_space_constraint(blocks, pltpu.HBM)
    hbm = whole(pltpu.HBM)
    return pl.pallas_call(
        fill_kernel,
        out_shape=[
            jax.ShapeDtypeStruct((SLABS * chunk, rows, LANES), jnp.bfloat16),
            jax.ShapeDtypeStruct((2 * count,), jnp.int32),
            jax.ShapeDtypeStruct((rows, LANES), jnp.float32),
        ],
        in_specs=[hbm, hbm, hbm],
        out_specs=[VMEM, SMEM, VMEM],
        scratch_shapes=[
            pltpu.SMEM(pairs.shape, jnp.int32),
            pltpu.SMEM(table.shape, jnp.int32),
            pltpu.VMEM(blocks.shape, jnp.bfloat16),
            pltpu.SMEM((SLABS,), jnp.int32),
            pltpu.SMEM((2 * count,), jnp.int32),
            pltpu.SemaphoreType.DMA((3,)),
        ],
        compiler_params=params(),
    )(pairs, table, blocks)


def chunk_base(message, per_slab, tiles):
    place, rank = lax.div(message, per_slab), lax.rem(message, per_slab)
    first = place * (per_slab * tiles + 1)
    return first + rank * tiles, first + per_slab * tiles, rank


def sort_kernel(origin_ref, arrived_ref, *out_refs):
    size, _, features = out_refs[0].shape
    tiles = features // LANES
    per_slab = len(GROUPS) * size // SLABS
    chunked = arrived_ref.shape[2] != features
    for place, out_ref in enumerate(out_refs):

        def body(index, carry, place=place, out_ref=out_ref):
            origin = origin_ref[place * size + index]
            if not chunked:
                out_ref[index] = arrived_ref[origin]
                return carry
            base, _, _ = chunk_base(origin, per_slab, tiles)
            for tile in range(tiles):
                out_ref[index, :, tile * LANES : (tile + 1) * LANES] = arrived_ref[base + tile]
            return carry

        lax.fori_loop(0, size, body, 0, unroll=16)


def sort_by_depth(arrived, origin, features):
    total, rows = origin.shape[0], arrived.shape[1]
    part = jax.ShapeDtypeStruct((total // len(GROUPS), rows, features), jnp.bfloat16)
    return pl.pallas_call(
        sort_kernel,
        out_shape=[part] * len(GROUPS),
        in_specs=[SMEM, VMEM],
        out_specs=[VMEM] * len(GROUPS),
        compiler_params=params(),
    )(origin, arrived)


def unsort_kernel(origin_ref, *refs):
    part_refs, out_ref, logs_ref = refs[:-2], refs[-2], refs[-1]
    size, rows, features = part_refs[0].shape
    size -= 1
    tiles = features // LANES
    total = len(GROUPS) * size
    per_slab = total // SLABS
    lane = lax.broadcasted_iota(jnp.int32, (rows, LANES), 1)
    halves = [lane < LANES // 2, lane >= LANES // 2]
    for place, part_ref in enumerate(part_refs):
        for index in range(size):
            origin = origin_ref[place * size + index]
            base, _, _ = chunk_base(origin, per_slab, tiles)
            for tile in range(tiles):
                out_ref[base + tile] = part_ref[index, :, tile * LANES : (tile + 1) * LANES]
            first = index // 2 * LANES
            terms = part_ref[size, :, first : first + LANES].astype(jnp.float32)
            logs_ref[origin] = jnp.where(halves[index % 2], terms, 0.0)
    slot = lane % (LANES // 2) // TERM_LANES

    def pack(place, carry):
        tile = logs_ref[place * per_slab]
        for rank in range(1, per_slab):
            tile = jnp.where(slot == rank, logs_ref[place * per_slab + rank], tile)
        out_ref[place * (per_slab * tiles + 1) + per_slab * tiles] = tile.astype(jnp.bfloat16)
        return carry

    lax.fori_loop(0, SLABS, pack, 0, unroll=16)


def unsort(parts, origin):
    size, rows, features = parts[0].shape
    total = origin.shape[0]
    chunk = total // SLABS * (features // LANES) + 1
    return pl.pallas_call(
        unsort_kernel,
        out_shape=jax.ShapeDtypeStruct((SLABS * chunk, rows, LANES), jnp.bfloat16),
        in_specs=[SMEM] + [VMEM] * len(GROUPS),
        out_specs=VMEM,
        scratch_shapes=[pltpu.VMEM((total, rows, LANES), jnp.float32)],
        compiler_params=params(),
    )(origin, *parts)


def products_of(flat, cluster):
    return lax.dot_general(
        flat, cluster, (((1,), (1,)), ((), ())), preferred_element_type=jnp.float32
    )


def weigh(products, norms):
    scores = (products - norms) * INV_WIDTH
    row_top = jnp.max(scores, axis=1, keepdims=True)
    weights = jnp.exp(scores - row_top)
    totals = jnp.sum(weights, axis=1, keepdims=True)
    log_weight = row_top + jnp.log(totals)
    first = log_weight.astype(jnp.bfloat16).astype(jnp.float32)
    rest = log_weight - first
    second = rest.astype(jnp.bfloat16).astype(jnp.float32)
    third = rest - second
    lane = lax.broadcasted_iota(jnp.int32, (products.shape[0], LANES), 1) % TERM_LANES
    terms = jnp.where(lane == 0, first, jnp.where(lane == 1, second, third))
    return weights.astype(jnp.bfloat16), totals, terms


def score_kernel(*refs):
    count = len(GROUPS)
    part_refs, refs = refs[:count], refs[count:]
    cluster_anys, refs = refs[:count], refs[count:]
    norm_refs, refs = refs[:count], refs[count:]
    out_refs, (clusters_ref, cluster_sems) = refs[:count], refs[count:]
    copies = [
        pltpu.make_async_copy(cluster_any, clusters_ref.at[index], cluster_sems.at[index])
        for index, cluster_any in enumerate(cluster_anys)
    ]
    for copy in copies:
        copy.start()
    size, rows, features = part_refs[0].shape
    half = size // 2
    lines = half * rows
    first_half = lax.broadcasted_iota(jnp.int32, (rows, LANES), 1) < LANES // 2
    members = [
        [(group, side) for group, pair in enumerate(GROUPS) for side in range(2) if pair[side] == cluster]
        for cluster in range(count)
    ]
    products = []
    for cluster in range(count):
        flat = jnp.concatenate(
            [
                part_refs[group][side * half : (side + 1) * half]
                .astype(jnp.float32)
                .reshape(lines, features)
                for group, side in members[cluster]
            ]
        ).astype(jnp.bfloat16)
        copies[cluster].wait()
        products.append(products_of(flat, clusters_ref[cluster]))
    for cluster in range(count):
        weights, totals, terms = weigh(products[cluster], norm_refs[cluster][...])
        summed = jnp.dot(weights, clusters_ref[cluster], preferred_element_type=jnp.float32)
        part = summed * (1.0 / totals)
        for place, (group, side) in enumerate(members[cluster]):
            first, out_ref = place * lines, out_refs[group]
            out_ref[side * half : (side + 1) * half] = (
                part[first : first + lines].reshape(half, rows, features).astype(jnp.bfloat16)
            )
            for index in range(0, half, 2):
                line = first + index * rows
                both = jnp.where(
                    first_half, terms[line : line + rows], terms[line + rows : line + 2 * rows]
                )
                lanes = (side * half + index) // 2 * LANES
                out_ref[size, :, lanes : lanes + LANES] = both.astype(jnp.bfloat16)


def score_parts(parts, clusters, norms):
    count = len(GROUPS)
    size, rows, features = parts[0].shape
    references = clusters[0].shape[0]
    total = count * size * rows
    out = jax.ShapeDtypeStruct((size + 1, rows, features), jnp.bfloat16)
    return pl.pallas_call(
        score_kernel,
        out_shape=[out] * count,
        in_specs=[VMEM] * count + [whole(pl.ANY)] * count + [VMEM] * count,
        out_specs=[VMEM] * count,
        scratch_shapes=[
            pltpu.VMEM((count, references, features), jnp.bfloat16),
            pltpu.SemaphoreType.DMA((count,)),
        ],
        compiler_params=params(),
        cost_estimate=pl.CostEstimate(
            flops=4 * total * references * features,
            bytes_accessed=2 * (2 * total * features + count * references * features),
            transcendentals=total * references,
        ),
    )(*parts, *clusters, *norms)


def combine_kernel(log_count, step, slots_ref, squares_ref, returned_ref, earlier_ref, *out_refs):
    density_ref, *out_refs = out_refs
    rows = squares_ref.shape[0]
    count = slots_ref.shape[0] // 2
    per_slab = 2 * count // SLABS
    tiles = (returned_ref.shape[0] // SLABS - 1) // per_slab
    row = lax.broadcasted_iota(jnp.int32, (rows, LANES), 0)
    lane = lax.broadcasted_iota(jnp.int32, (rows, LANES), 1)
    lane_slot = jnp.where(
        lane % TERM_LANES < TERMS, lane % (LANES // 2) // TERM_LANES, -1
    )
    last = len(out_refs) == 1
    squares = squares_ref[...]

    def read(slot):
        base, shared, rank = chunk_base(slot, per_slab, tiles)
        part = returned_ref[pl.ds(base, tiles)].astype(jnp.float32)
        terms = returned_ref[shared].astype(jnp.float32)
        terms = jnp.where(lane_slot == rank, terms, 0.0)
        return part, jnp.sum(terms, axis=1, keepdims=True)

    def body(block, carry):
        densities, next_squares = carry
        first_slot, second_slot = slots_ref[2 * block], slots_ref[2 * block + 1]
        first_part, first_log = read(first_slot)
        second_part, second_log = read(second_slot)
        both_top = jnp.maximum(first_log, second_log)
        first_share = jnp.exp(first_log - both_top)
        second_share = jnp.exp(second_log - both_top)
        pair_total = first_share + second_share
        inverse = 1.0 / pair_total
        mixed = (
            (first_share * inverse)[None] * first_part
            + (second_share * inverse)[None] * second_part
        ).astype(jnp.bfloat16)
        density = both_top + jnp.log(pair_total)
        densities = jnp.where(lane == block, density, densities)
        if last:
            for tile in range(tiles):
                out_refs[0][block, :, tile * LANES : (tile + 1) * LANES] = mixed[tile]
            return densities, next_squares
        for tile in range(tiles):
            lanes = slice(tile * LANES, (tile + 1) * LANES)
            out_refs[0][first_slot, :, lanes] = mixed[tile]
            out_refs[0][second_slot, :, lanes] = mixed[tile]
        total = jnp.sum(jnp.square(mixed.astype(jnp.float32)), axis=0)
        total = jnp.sum(total, axis=1, keepdims=True)
        return densities, jnp.where(lane == block, total, next_squares)

    zeros = jnp.zeros((rows, LANES), jnp.float32)
    densities, next_squares = lax.fori_loop(0, count, body, (zeros, zeros), unroll=16)
    if not last:
        out_refs[1][...] = next_squares
    densities = densities - 0.5 * INV_WIDTH * squares - log_count
    blocks_wide = LANES // rows
    for wide in range(count // blocks_wide):
        spread = zeros
        for index in range(blocks_wide):
            block = wide * blocks_wide + index
            column = densities[:, block : block + 1]
            spread = jnp.where(lane == index * rows + row, column, spread)
        line = jnp.sum(
            jnp.where(lane % rows == row, spread, 0.0), axis=0, keepdims=True
        )
        lanes = slice(wide * LANES, (wide + 1) * LANES)
        for other in range(density_ref.shape[0]):
            if other == step:
                density_ref[other : other + 1, lanes] = line
            else:
                density_ref[other : other + 1, lanes] = earlier_ref[other : other + 1, lanes]


def combine(squares, returned, slots, earlier, log_count, step, features):
    rows = squares.shape[0]
    total = slots.shape[0]
    outs = [jax.ShapeDtypeStruct(earlier.shape, jnp.float32)]
    if step == STEPS - 1:
        outs.append(jax.ShapeDtypeStruct((total // 2, rows, features), jnp.bfloat16))
    else:
        outs.append(jax.ShapeDtypeStruct((total, rows, features), jnp.bfloat16))
        outs.append(jax.ShapeDtypeStruct(squares.shape, jnp.float32))
    return pl.pallas_call(
        functools.partial(combine_kernel, log_count, step),
        out_shape=outs,
        in_specs=[SMEM, VMEM, VMEM, VMEM],
        out_specs=[VMEM] * len(outs),
        compiler_params=params(),
    )(slots, squares, returned, earlier)


def half_norms_of(cluster_rows):
    return 0.5 * jnp.sum(jnp.square(cluster_rows.astype(jnp.float32)), axis=1)[None, :]


def sorted_origins(arrived, total, depth, core):
    chunks = arrived.reshape(SLABS, -1, *arrived.shape[1:])
    targets = chunks[:, -1, 0, : total // SLABS].reshape(-1).astype(jnp.int32)
    order = jnp.arange(total, dtype=jnp.int32)
    earlier = (targets[:, None] == targets[None, :]) & (order[None, :] < order[:, None])
    rank = jnp.sum(earlier.astype(jnp.int32), axis=1)
    side = (targets % CORES) ^ core
    ahead = targets // CORES - depth
    ahead = jnp.where(core == 0, ahead, -ahead) % DEPTH
    half = sum(
        jnp.where((side == at) & (ahead == steps), HALVES[at][steps], 0)
        for at in range(CORES)
        for steps in range(DEPTH)
    )
    slot = half * (total // CLUSTER_DEVICES) + rank
    return jnp.sum(jnp.where(slot[None, :] == order[:, None], order[None, :], 0), axis=1)


def local(queries, corpus, block_pairs, owner_table):
    features = queries.shape[2]
    cluster_index = lax.axis_index("cluster").astype(jnp.int32)
    depth, core = cluster_index // CORES, cluster_index % CORES
    own = corpus[0]
    ahead = send_ahead(own, -1)
    other = swap_cores(own)
    log_count = math.log(2.0 * own.shape[0])
    outgoing, slots, squares = fill(queries, block_pairs.T, owner_table)
    densities = jnp.zeros((STEPS, queries.shape[0] * queries.shape[1]), jnp.float32)
    for step in range(STEPS):
        arrived = exchange_slabs(outgoing)
        if step == 0:
            origin = sorted_origins(arrived, slots.shape[0], depth, core)
        parts = list(sort_by_depth(arrived, origin, features))
        if step == 0:
            ahead, parts[0] = lax.optimization_barrier((ahead, parts[0]))
            clusters = (own, other, ahead, swap_cores(ahead))
            norms = [half_norms_of(cluster) for cluster in clusters]
        parts[STAY:] = [send_ahead(parts[STAY], 1), send_ahead(parts[STAY + 1], -1)]
        answers = list(score_parts(parts, clusters, norms))
        answers[STAY:] = [send_ahead(answers[STAY], -1), send_ahead(answers[STAY + 1], 1)]
        returned = exchange_slabs(unsort(answers, origin))
        densities, outgoing, *squares_next = combine(
            squares, returned, slots, densities, log_count, step, features
        )
        squares = squares_next[0] if squares_next else None
    return (outgoing, densities)


def solution(mesh):
    return jax.shard_map(
        local,
        mesh=mesh,
        in_specs=(
            P(("cluster", "slab"), None, None),
            P(("cluster", "slab"), None, None),
            P(("cluster", "slab"), None),
            P(),
        ),
        out_specs=(P(("cluster", "slab"), None, None), P(None, ("cluster", "slab"))),
        check_vma=False,
    )
```

```python
import functools
import math

import jax
import jax.numpy as jnp
from jax import lax
from jax.experimental import pallas as pl
from jax.experimental.pallas import tpu as pltpu
from jax.sharding import PartitionSpec as P

STEPS = 2
INV_WIDTH = 1.0 / 16.0
LANES = 128
VMEM_LIMIT = 48 * 1024 * 1024
AXES = ("cluster", "slab")
SIDE = 4
CORES = 2
DEPTH = 4
SLABS = SIDE * SIDE
CLUSTER_DEVICES = DEPTH * CORES
OWN, OTHER, AHEAD, OTHER_AHEAD = range(4)
GROUPS = ((OWN, OTHER), (AHEAD, OTHER_AHEAD), (AHEAD, OTHER), (OWN, OTHER_AHEAD))
STAY = 2
HALVES = ((0, 2, 4, 6), (1, 5, 7, 3))
TERM_LANES = 8
TERMS = 3


def slab_order(core):
    return [2, 10, 0, 14, 6, 5, 3, 8, 7, 11, 15, 1, 12, 13, 9, 4] if core == 0 else [2, 3, 11, 10, 8, 1, 5, 4, 7, 15, 9, 12, 6, 13, 14, 0]


def slab_groups():
    return [
        [cluster * SLABS + slab for slab in slab_order(cluster % CORES)]
        for cluster in range(CLUSTER_DEVICES)
    ]


def exchange_slabs(array):
    return lax.all_to_all(
        array, AXES, split_axis=0, concat_axis=0, tiled=True, axis_index_groups=slab_groups()
    )


def send_ahead(array, steps):
    pairs = []
    for z in range(DEPTH):
        for core in range(CORES):
            target_z = (z + (steps if core == 0 else -steps)) % DEPTH
            for slab in range(SLABS):
                source = (z * CORES + core) * SLABS + slab
                target = (target_z * CORES + core) * SLABS + slab
                pairs.append((source, target))
    return lax.ppermute(array, AXES, pairs)


def swap_cores(array):
    pairs = []
    for cluster in range(CLUSTER_DEVICES):
        for slab in range(SLABS):
            pairs.append((cluster * SLABS + slab, (cluster ^ 1) * SLABS + slab))
    return lax.ppermute(array, AXES, pairs)


def whole(space):
    return pl.BlockSpec(memory_space=space)


SMEM, VMEM = whole(pltpu.SMEM), whole(pltpu.VMEM)


def params():
    return pltpu.CompilerParams(vmem_limit_bytes=VMEM_LIMIT)


def slab_places(core):
    order = slab_order(core)
    return [order.index(slab) for slab in range(SLABS)]


def fill_kernel(
    pairs_hbm, table_hbm, blocks_hbm, out_ref, slots_ref, squares_ref,
    pairs_ref, table_ref, blocks_ref, places_ref, counts_ref, targets_ref, input_sems,
):
    count, rows, features = blocks_ref.shape
    tiles = features // LANES
    per_slab = 2 * count // SLABS
    core = lax.rem(lax.axis_index("cluster").astype(jnp.int32), CORES)
    inputs = [
        pltpu.make_async_copy(pairs_hbm, pairs_ref, input_sems.at[0]),
        pltpu.make_async_copy(table_hbm, table_ref, input_sems.at[1]),
        pltpu.make_async_copy(blocks_hbm, blocks_ref, input_sems.at[2]),
    ]
    for copy in inputs:
        copy.start()
    for slab, (first, second) in enumerate(zip(slab_places(0), slab_places(1))):
        places_ref[slab] = jnp.where(core == 0, first, second)
        counts_ref[slab] = 0
    for copy in inputs[:2]:
        copy.wait()

    def assign(block, carry):
        for side in range(2):
            entry = table_ref[pairs_ref[side, block]]
            place = places_ref[lax.rem(entry, SLABS)]
            rank = counts_ref[place]
            counts_ref[place] = rank + 1
            slot = place * per_slab + rank
            slots_ref[2 * block + side] = slot
            targets_ref[slot] = lax.div(entry, SLABS)
        return carry

    lax.fori_loop(0, count, assign, 0, unroll=32)
    inputs[2].wait()
    lane = lax.broadcasted_iota(jnp.int32, (rows, LANES), 1)

    def put(block, squares):
        bases = [chunk_base(slots_ref[2 * block + side], per_slab, tiles)[0] for side in range(2)]
        total = jnp.zeros((rows, LANES), jnp.float32)
        for tile in range(tiles):
            values = blocks_ref[block, :, tile * LANES : (tile + 1) * LANES]
            for base in bases:
                out_ref[base + tile] = values
            total += jnp.square(values.astype(jnp.float32))
        return jnp.where(lane == block, jnp.sum(total, axis=1, keepdims=True), squares)

    squares_ref[...] = lax.fori_loop(
        0, count, put, jnp.zeros((rows, LANES), jnp.float32), unroll=32
    )

    def note(place, carry):
        tile = jnp.zeros((rows, LANES), jnp.int32)
        for rank in range(per_slab):
            tile = jnp.where(lane == rank, targets_ref[place * per_slab + rank], tile)
        tile = tile.astype(jnp.float32).astype(jnp.bfloat16)
        out_ref[place * (per_slab * tiles + 1) + per_slab * tiles] = tile
        return carry

    lax.fori_loop(0, SLABS, note, 0, unroll=16)


def fill(blocks, pairs, table):
    count, rows, features = blocks.shape
    chunk = 2 * count // SLABS * (features // LANES) + 1
    pairs = pltpu.with_memory_space_constraint(pairs, pltpu.HBM)
    table = pltpu.with_memory_space_constraint(table, pltpu.HBM)
    blocks = pltpu.with_memory_space_constraint(blocks, pltpu.HBM)
    hbm = whole(pltpu.HBM)
    return pl.pallas_call(
        fill_kernel,
        out_shape=[
            jax.ShapeDtypeStruct((SLABS * chunk, rows, LANES), jnp.bfloat16),
            jax.ShapeDtypeStruct((2 * count,), jnp.int32),
            jax.ShapeDtypeStruct((rows, LANES), jnp.float32),
        ],
        in_specs=[hbm, hbm, hbm],
        out_specs=[VMEM, SMEM, VMEM],
        scratch_shapes=[
            pltpu.SMEM(pairs.shape, jnp.int32),
            pltpu.SMEM(table.shape, jnp.int32),
            pltpu.VMEM(blocks.shape, jnp.bfloat16),
            pltpu.SMEM((SLABS,), jnp.int32),
            pltpu.SMEM((SLABS,), jnp.int32),
            pltpu.SMEM((2 * count,), jnp.int32),
            pltpu.SemaphoreType.DMA((3,)),
        ],
        compiler_params=params(),
    )(pairs, table, blocks)


def chunk_base(message, per_slab, tiles):
    place, rank = lax.div(message, per_slab), lax.rem(message, per_slab)
    first = place * (per_slab * tiles + 1)
    return first + rank * tiles, first + per_slab * tiles, rank


def sort_kernel(origin_ref, arrived_ref, *out_refs):
    size, _, features = out_refs[0].shape
    tiles = features // LANES
    per_slab = len(GROUPS) * size // SLABS
    chunked = arrived_ref.shape[2] != features
    for place, out_ref in enumerate(out_refs):

        def body(index, carry, place=place, out_ref=out_ref):
            origin = origin_ref[place * size + index]
            if not chunked:
                out_ref[index] = arrived_ref[origin]
                return carry
            base, _, _ = chunk_base(origin, per_slab, tiles)
            for tile in range(tiles):
                out_ref[index, :, tile * LANES : (tile + 1) * LANES] = arrived_ref[base + tile]
            return carry

        lax.fori_loop(0, size, body, 0, unroll=16)


def sort_by_depth(arrived, origin, features):
    total, rows = origin.shape[0], arrived.shape[1]
    part = jax.ShapeDtypeStruct((total // len(GROUPS), rows, features), jnp.bfloat16)
    return pl.pallas_call(
        sort_kernel,
        out_shape=[part] * len(GROUPS),
        in_specs=[SMEM, VMEM],
        out_specs=[VMEM] * len(GROUPS),
        compiler_params=params(),
    )(origin, arrived)


def unsort_kernel(origin_ref, *refs):
    part_refs, out_ref, logs_ref = refs[:-2], refs[-2], refs[-1]
    size, rows, features = part_refs[0].shape
    size -= 1
    tiles = features // LANES
    total = len(GROUPS) * size
    per_slab = total // SLABS
    lane = lax.broadcasted_iota(jnp.int32, (rows, LANES), 1)
    halves = [lane < LANES // 2, lane >= LANES // 2]
    for place, part_ref in enumerate(part_refs):
        for index in range(size):
            origin = origin_ref[place * size + index]
            base, _, _ = chunk_base(origin, per_slab, tiles)
            for tile in range(tiles):
                out_ref[base + tile] = part_ref[index, :, tile * LANES : (tile + 1) * LANES]
            first = index // 2 * LANES
            terms = part_ref[size, :, first : first + LANES].astype(jnp.float32)
            logs_ref[origin] = jnp.where(halves[index % 2], terms, 0.0)
    slot = lane % (LANES // 2) // TERM_LANES

    def pack(place, carry):
        tile = logs_ref[place * per_slab]
        for rank in range(1, per_slab):
            tile = jnp.where(slot == rank, logs_ref[place * per_slab + rank], tile)
        out_ref[place * (per_slab * tiles + 1) + per_slab * tiles] = tile.astype(jnp.bfloat16)
        return carry

    lax.fori_loop(0, SLABS, pack, 0, unroll=16)


def unsort(parts, origin):
    size, rows, features = parts[0].shape
    total = origin.shape[0]
    chunk = total // SLABS * (features // LANES) + 1
    return pl.pallas_call(
        unsort_kernel,
        out_shape=jax.ShapeDtypeStruct((SLABS * chunk, rows, LANES), jnp.bfloat16),
        in_specs=[SMEM] + [VMEM] * len(GROUPS),
        out_specs=VMEM,
        scratch_shapes=[pltpu.VMEM((total, rows, LANES), jnp.float32)],
        compiler_params=params(),
    )(origin, *parts)


def products_of(flat, cluster):
    return lax.dot_general(
        flat, cluster, (((1,), (1,)), ((), ())), preferred_element_type=jnp.float32
    )


def weigh(products, norms):
    scores = (products - norms) * INV_WIDTH
    row_top = jnp.max(scores, axis=1, keepdims=True)
    weights = jnp.exp(scores - row_top)
    totals = jnp.sum(weights, axis=1, keepdims=True)
    log_weight = row_top + jnp.log(totals)
    first = log_weight.astype(jnp.bfloat16).astype(jnp.float32)
    rest = log_weight - first
    second = rest.astype(jnp.bfloat16).astype(jnp.float32)
    third = rest - second
    lane = lax.broadcasted_iota(jnp.int32, (products.shape[0], LANES), 1) % TERM_LANES
    terms = jnp.where(lane == 0, first, jnp.where(lane == 1, second, third))
    return weights.astype(jnp.bfloat16), totals, terms


def score_kernel(*refs):
    count = len(GROUPS)
    part_refs, refs = refs[:count], refs[count:]
    cluster_anys, refs = refs[:count], refs[count:]
    norm_refs, refs = refs[:count], refs[count:]
    out_refs, (clusters_ref, cluster_sems) = refs[:count], refs[count:]
    copies = [
        pltpu.make_async_copy(cluster_any, clusters_ref.at[index], cluster_sems.at[index])
        for index, cluster_any in enumerate(cluster_anys)
    ]
    for copy in copies:
        copy.start()
    size, rows, features = part_refs[0].shape
    half = size // 2
    lines = half * rows
    first_half = lax.broadcasted_iota(jnp.int32, (rows, LANES), 1) < LANES // 2
    members = [
        [(group, side) for group, pair in enumerate(GROUPS) for side in range(2) if pair[side] == cluster]
        for cluster in range(count)
    ]
    products = []
    for cluster in range(count):
        flat = jnp.concatenate(
            [
                part_refs[group][side * half : (side + 1) * half]
                .astype(jnp.float32)
                .reshape(lines, features)
                for group, side in members[cluster]
            ]
        ).astype(jnp.bfloat16)
        copies[cluster].wait()
        products.append(products_of(flat, clusters_ref[cluster]))
    for cluster in range(count):
        weights, totals, terms = weigh(products[cluster], norm_refs[cluster][...])
        summed = jnp.dot(weights, clusters_ref[cluster], preferred_element_type=jnp.float32)
        part = summed * (1.0 / totals)
        for place, (group, side) in enumerate(members[cluster]):
            first, out_ref = place * lines, out_refs[group]
            out_ref[side * half : (side + 1) * half] = (
                part[first : first + lines].reshape(half, rows, features).astype(jnp.bfloat16)
            )
            for index in range(0, half, 2):
                line = first + index * rows
                both = jnp.where(
                    first_half, terms[line : line + rows], terms[line + rows : line + 2 * rows]
                )
                lanes = (side * half + index) // 2 * LANES
                out_ref[size, :, lanes : lanes + LANES] = both.astype(jnp.bfloat16)


def score_parts(parts, clusters, norms):
    count = len(GROUPS)
    size, rows, features = parts[0].shape
    references = clusters[0].shape[0]
    total = count * size * rows
    out = jax.ShapeDtypeStruct((size + 1, rows, features), jnp.bfloat16)
    return pl.pallas_call(
        score_kernel,
        out_shape=[out] * count,
        in_specs=[VMEM] * count + [whole(pl.ANY)] * count + [VMEM] * count,
        out_specs=[VMEM] * count,
        scratch_shapes=[
            pltpu.VMEM((count, references, features), jnp.bfloat16),
            pltpu.SemaphoreType.DMA((count,)),
        ],
        compiler_params=params(),
        cost_estimate=pl.CostEstimate(
            flops=4 * total * references * features,
            bytes_accessed=2 * (2 * total * features + count * references * features),
            transcendentals=total * references,
        ),
    )(*parts, *clusters, *norms)


def combine_kernel(log_count, step, slots_ref, squares_ref, returned_ref, earlier_ref, *out_refs):
    density_ref, *out_refs = out_refs
    rows = squares_ref.shape[0]
    count = slots_ref.shape[0] // 2
    per_slab = 2 * count // SLABS
    tiles = (returned_ref.shape[0] // SLABS - 1) // per_slab
    row = lax.broadcasted_iota(jnp.int32, (rows, LANES), 0)
    lane = lax.broadcasted_iota(jnp.int32, (rows, LANES), 1)
    lane_slot = jnp.where(
        lane % TERM_LANES < TERMS, lane % (LANES // 2) // TERM_LANES, -1
    )
    last = len(out_refs) == 1
    squares = squares_ref[...]

    def read(slot):
        base, shared, rank = chunk_base(slot, per_slab, tiles)
        part = returned_ref[pl.ds(base, tiles)].astype(jnp.float32)
        terms = returned_ref[shared].astype(jnp.float32)
        terms = jnp.where(lane_slot == rank, terms, 0.0)
        return part, jnp.sum(terms, axis=1, keepdims=True)

    def body(block, carry):
        densities, next_squares = carry
        first_slot, second_slot = slots_ref[2 * block], slots_ref[2 * block + 1]
        first_part, first_log = read(first_slot)
        second_part, second_log = read(second_slot)
        both_top = jnp.maximum(first_log, second_log)
        first_share = jnp.exp(first_log - both_top)
        second_share = jnp.exp(second_log - both_top)
        pair_total = first_share + second_share
        inverse = 1.0 / pair_total
        mixed = (
            (first_share * inverse)[None] * first_part
            + (second_share * inverse)[None] * second_part
        ).astype(jnp.bfloat16)
        density = both_top + jnp.log(pair_total)
        densities = jnp.where(lane == block, density, densities)
        if last:
            for tile in range(tiles):
                out_refs[0][block, :, tile * LANES : (tile + 1) * LANES] = mixed[tile]
            return densities, next_squares
        for tile in range(tiles):
            lanes = slice(tile * LANES, (tile + 1) * LANES)
            out_refs[0][first_slot, :, lanes] = mixed[tile]
            out_refs[0][second_slot, :, lanes] = mixed[tile]
        total = jnp.sum(jnp.square(mixed.astype(jnp.float32)), axis=0)
        total = jnp.sum(total, axis=1, keepdims=True)
        return densities, jnp.where(lane == block, total, next_squares)

    zeros = jnp.zeros((rows, LANES), jnp.float32)
    densities, next_squares = lax.fori_loop(0, count, body, (zeros, zeros), unroll=32)
    if not last:
        out_refs[1][...] = next_squares
    densities = densities - 0.5 * INV_WIDTH * squares - log_count
    blocks_wide = LANES // rows
    for wide in range(count // blocks_wide):
        spread = zeros
        for index in range(blocks_wide):
            block = wide * blocks_wide + index
            column = densities[:, block : block + 1]
            spread = jnp.where(lane == index * rows + row, column, spread)
        line = jnp.sum(
            jnp.where(lane % rows == row, spread, 0.0), axis=0, keepdims=True
        )
        lanes = slice(wide * LANES, (wide + 1) * LANES)
        for other in range(density_ref.shape[0]):
            if other == step:
                density_ref[other : other + 1, lanes] = line
            else:
                density_ref[other : other + 1, lanes] = earlier_ref[other : other + 1, lanes]


def combine(squares, returned, slots, earlier, log_count, step, features):
    rows = squares.shape[0]
    total = slots.shape[0]
    outs = [jax.ShapeDtypeStruct(earlier.shape, jnp.float32)]
    if step == STEPS - 1:
        outs.append(jax.ShapeDtypeStruct((total // 2, rows, features), jnp.bfloat16))
    else:
        outs.append(jax.ShapeDtypeStruct((total, rows, features), jnp.bfloat16))
        outs.append(jax.ShapeDtypeStruct(squares.shape, jnp.float32))
    return pl.pallas_call(
        functools.partial(combine_kernel, log_count, step),
        out_shape=outs,
        in_specs=[SMEM, VMEM, VMEM, VMEM],
        out_specs=[VMEM] * len(outs),
        compiler_params=params(),
    )(slots, squares, returned, earlier)


def half_norms_of(cluster_rows):
    return 0.5 * jnp.sum(jnp.square(cluster_rows.astype(jnp.float32)), axis=1)[None, :]


def sorted_origins(arrived, total, depth, core):
    chunks = arrived.reshape(SLABS, -1, *arrived.shape[1:])
    targets = chunks[:, -1, 0, : total // SLABS].reshape(-1).astype(jnp.int32)
    order = jnp.arange(total, dtype=jnp.int32)
    earlier = (targets[:, None] == targets[None, :]) & (order[None, :] < order[:, None])
    rank = jnp.sum(earlier.astype(jnp.int32), axis=1)
    side = (targets % CORES) ^ core
    ahead = targets // CORES - depth
    ahead = jnp.where(core == 0, ahead, -ahead) % DEPTH
    half = sum(
        jnp.where((side == at) & (ahead == steps), HALVES[at][steps], 0)
        for at in range(CORES)
        for steps in range(DEPTH)
    )
    slot = half * (total // CLUSTER_DEVICES) + rank
    return jnp.sum(jnp.where(slot[None, :] == order[:, None], order[None, :], 0), axis=1)


def local(queries, corpus, block_pairs, owner_table):
    features = queries.shape[2]
    cluster_index = lax.axis_index("cluster").astype(jnp.int32)
    depth, core = cluster_index // CORES, cluster_index % CORES
    own = corpus[0]
    ahead = send_ahead(own, -1)
    other = swap_cores(own)
    log_count = math.log(2.0 * own.shape[0])
    outgoing, slots, squares = fill(queries, block_pairs.T, owner_table)
    densities = jnp.zeros((STEPS, queries.shape[0] * queries.shape[1]), jnp.float32)
    for step in range(STEPS):
        arrived = exchange_slabs(outgoing)
        if step == 0:
            origin = sorted_origins(arrived, slots.shape[0], depth, core)
        parts = list(sort_by_depth(arrived, origin, features))
        if step == 0:
            ahead, parts[0] = lax.optimization_barrier((ahead, parts[0]))
            clusters = (own, other, ahead, swap_cores(ahead))
            norms = [half_norms_of(cluster) for cluster in clusters]
        parts[STAY:] = [send_ahead(parts[STAY], 1), send_ahead(parts[STAY + 1], -1)]
        answers = list(score_parts(parts, clusters, norms))
        answers[STAY:] = [send_ahead(answers[STAY], -1), send_ahead(answers[STAY + 1], 1)]
        returned = exchange_slabs(unsort(answers, origin))
        densities, outgoing, *squares_next = combine(
            squares, returned, slots, densities, log_count, step, features
        )
        squares = squares_next[0] if squares_next else None
    return (outgoing, densities)


def solution(mesh):
    return jax.shard_map(
        local,
        mesh=mesh,
        in_specs=(
            P(("cluster", "slab"), None, None),
            P(("cluster", "slab"), None, None),
            P(("cluster", "slab"), None),
            P(),
        ),
        out_specs=(P(("cluster", "slab"), None, None), P(None, ("cluster", "slab"))),
        check_vma=False,
    )
```

```python
import functools
import math

import jax
import jax.numpy as jnp
from jax import lax
from jax.experimental import pallas as pl
from jax.experimental.pallas import tpu as pltpu
from jax.sharding import PartitionSpec as P

STEPS = 2
INV_WIDTH = 1.0 / 16.0
LANES = 128
VMEM_LIMIT = 48 * 1024 * 1024
AXES = ("cluster", "slab")
SIDE = 4
CORES = 2
DEPTH = 4
SLABS = SIDE * SIDE
CLUSTER_DEVICES = DEPTH * CORES
OWN, OTHER, AHEAD, OTHER_AHEAD = range(4)
GROUPS = ((OWN, OTHER), (AHEAD, OTHER_AHEAD), (AHEAD, OTHER), (OWN, OTHER_AHEAD))
STAY = 2
HALVES = ((0, 2, 4, 6), (1, 5, 7, 3))
TERM_LANES = 8
TERMS = 3


def slab_order(core):
    return [2, 10, 0, 14, 6, 5, 3, 8, 7, 11, 15, 1, 12, 13, 9, 4] if core == 0 else [2, 3, 11, 10, 8, 1, 5, 4, 7, 15, 9, 12, 6, 13, 14, 0]


def slab_groups():
    return [
        [cluster * SLABS + slab for slab in slab_order(cluster % CORES)]
        for cluster in range(CLUSTER_DEVICES)
    ]


def exchange_slabs(array):
    return lax.all_to_all(
        array, AXES, split_axis=0, concat_axis=0, tiled=True, axis_index_groups=slab_groups()
    )


def send_ahead(array, steps):
    pairs = []
    for z in range(DEPTH):
        for core in range(CORES):
            target_z = (z + (steps if core == 0 else -steps)) % DEPTH
            for slab in range(SLABS):
                source = (z * CORES + core) * SLABS + slab
                target = (target_z * CORES + core) * SLABS + slab
                pairs.append((source, target))
    return lax.ppermute(array, AXES, pairs)


def swap_cores(array):
    pairs = []
    for cluster in range(CLUSTER_DEVICES):
        for slab in range(SLABS):
            pairs.append((cluster * SLABS + slab, (cluster ^ 1) * SLABS + slab))
    return lax.ppermute(array, AXES, pairs)


def whole(space):
    return pl.BlockSpec(memory_space=space)


SMEM, VMEM = whole(pltpu.SMEM), whole(pltpu.VMEM)


def params():
    return pltpu.CompilerParams(vmem_limit_bytes=VMEM_LIMIT)


def slab_places(core):
    order = slab_order(core)
    return [order.index(slab) for slab in range(SLABS)]


def fill_kernel(
    pairs_hbm, table_hbm, blocks_hbm, out_ref, slots_ref, squares_ref,
    pairs_ref, table_ref, blocks_ref, places_ref, counts_ref, targets_ref, input_sems,
):
    count, rows, features = blocks_ref.shape
    tiles = features // LANES
    per_slab = 2 * count // SLABS
    core = lax.rem(lax.axis_index("cluster").astype(jnp.int32), CORES)
    inputs = [
        pltpu.make_async_copy(pairs_hbm, pairs_ref, input_sems.at[0]),
        pltpu.make_async_copy(table_hbm, table_ref, input_sems.at[1]),
        pltpu.make_async_copy(blocks_hbm, blocks_ref, input_sems.at[2]),
    ]
    for copy in inputs:
        copy.start()
    for slab, (first, second) in enumerate(zip(slab_places(0), slab_places(1))):
        places_ref[slab] = jnp.where(core == 0, first, second)
        counts_ref[slab] = 0
    for copy in inputs[:2]:
        copy.wait()

    def assign(block, carry):
        for side in range(2):
            entry = table_ref[pairs_ref[side, block]]
            place = places_ref[lax.rem(entry, SLABS)]
            rank = counts_ref[place]
            counts_ref[place] = rank + 1
            slot = place * per_slab + rank
            slots_ref[2 * block + side] = slot
            targets_ref[slot] = lax.div(entry, SLABS)
        return carry

    lax.fori_loop(0, count, assign, 0, unroll=32)
    inputs[2].wait()
    lane = lax.broadcasted_iota(jnp.int32, (rows, LANES), 1)

    def put(block, squares):
        bases = [chunk_base(slots_ref[2 * block + side], per_slab, tiles)[0] for side in range(2)]
        total = jnp.zeros((rows, LANES), jnp.float32)
        for tile in range(tiles):
            values = blocks_ref[block, :, tile * LANES : (tile + 1) * LANES]
            for base in bases:
                out_ref[base + tile] = values
            total += jnp.square(values.astype(jnp.float32))
        return jnp.where(lane == block, jnp.sum(total, axis=1, keepdims=True), squares)

    squares_ref[...] = lax.fori_loop(
        0, count, put, jnp.zeros((rows, LANES), jnp.float32), unroll=32
    )

    def note(place, carry):
        tile = jnp.zeros((rows, LANES), jnp.int32)
        for rank in range(per_slab):
            tile = jnp.where(lane == rank, targets_ref[place * per_slab + rank], tile)
        tile = tile.astype(jnp.float32).astype(jnp.bfloat16)
        out_ref[place * (per_slab * tiles + 1) + per_slab * tiles] = tile
        return carry

    lax.fori_loop(0, SLABS, note, 0, unroll=16)


def fill(blocks, pairs, table):
    count, rows, features = blocks.shape
    chunk = 2 * count // SLABS * (features // LANES) + 1
    pairs = pltpu.with_memory_space_constraint(pairs, pltpu.HBM)
    table = pltpu.with_memory_space_constraint(table, pltpu.HBM)
    blocks = pltpu.with_memory_space_constraint(blocks, pltpu.HBM)
    hbm = whole(pltpu.HBM)
    return pl.pallas_call(
        fill_kernel,
        out_shape=[
            jax.ShapeDtypeStruct((SLABS * chunk, rows, LANES), jnp.bfloat16),
            jax.ShapeDtypeStruct((2 * count,), jnp.int32),
            jax.ShapeDtypeStruct((rows, LANES), jnp.float32),
        ],
        in_specs=[hbm, hbm, hbm],
        out_specs=[VMEM, SMEM, VMEM],
        scratch_shapes=[
            pltpu.SMEM(pairs.shape, jnp.int32),
            pltpu.SMEM(table.shape, jnp.int32),
            pltpu.VMEM(blocks.shape, jnp.bfloat16),
            pltpu.SMEM((SLABS,), jnp.int32),
            pltpu.SMEM((SLABS,), jnp.int32),
            pltpu.SMEM((2 * count,), jnp.int32),
            pltpu.SemaphoreType.DMA((3,)),
        ],
        compiler_params=params(),
    )(pairs, table, blocks)


def chunk_base(message, per_slab, tiles):
    place, rank = lax.div(message, per_slab), lax.rem(message, per_slab)
    first = place * (per_slab * tiles + 1)
    return first + rank * tiles, first + per_slab * tiles, rank


def sort_kernel(origin_ref, arrived_ref, *out_refs):
    size, _, features = out_refs[0].shape
    tiles = features // LANES
    per_slab = len(GROUPS) * size // SLABS
    chunked = arrived_ref.shape[2] != features
    for place, out_ref in enumerate(out_refs):

        def body(index, carry, place=place, out_ref=out_ref):
            origin = origin_ref[place * size + index]
            if not chunked:
                out_ref[index] = arrived_ref[origin]
                return carry
            base, _, _ = chunk_base(origin, per_slab, tiles)
            for tile in range(tiles):
                out_ref[index, :, tile * LANES : (tile + 1) * LANES] = arrived_ref[base + tile]
            return carry

        lax.fori_loop(0, size, body, 0, unroll=16)


def sort_by_depth(arrived, origin, features):
    total, rows = origin.shape[0], arrived.shape[1]
    part = jax.ShapeDtypeStruct((total // len(GROUPS), rows, features), jnp.bfloat16)
    return pl.pallas_call(
        sort_kernel,
        out_shape=[part] * len(GROUPS),
        in_specs=[SMEM, VMEM],
        out_specs=[VMEM] * len(GROUPS),
        compiler_params=params(),
    )(origin, arrived)


def unsort_kernel(origin_ref, *refs):
    part_refs, out_ref, logs_ref = refs[:-2], refs[-2], refs[-1]
    size, rows, features = part_refs[0].shape
    size -= 1
    tiles = features // LANES
    total = len(GROUPS) * size
    per_slab = total // SLABS
    lane = lax.broadcasted_iota(jnp.int32, (rows, LANES), 1)
    halves = [lane < LANES // 2, lane >= LANES // 2]
    for place, part_ref in enumerate(part_refs):
        for index in range(size):
            origin = origin_ref[place * size + index]
            base, _, _ = chunk_base(origin, per_slab, tiles)
            for tile in range(tiles):
                out_ref[base + tile] = part_ref[index, :, tile * LANES : (tile + 1) * LANES]
            first = index // 2 * LANES
            terms = part_ref[size, :, first : first + LANES].astype(jnp.float32)
            logs_ref[origin] = jnp.where(halves[index % 2], terms, 0.0)
    slot = lane % (LANES // 2) // TERM_LANES

    def pack(place, carry):
        tile = logs_ref[place * per_slab]
        for rank in range(1, per_slab):
            tile = jnp.where(slot == rank, logs_ref[place * per_slab + rank], tile)
        out_ref[place * (per_slab * tiles + 1) + per_slab * tiles] = tile.astype(jnp.bfloat16)
        return carry

    lax.fori_loop(0, SLABS, pack, 0, unroll=16)


def unsort(parts, origin):
    size, rows, features = parts[0].shape
    total = origin.shape[0]
    chunk = total // SLABS * (features // LANES) + 1
    return pl.pallas_call(
        unsort_kernel,
        out_shape=jax.ShapeDtypeStruct((SLABS * chunk, rows, LANES), jnp.bfloat16),
        in_specs=[SMEM] + [VMEM] * len(GROUPS),
        out_specs=VMEM,
        scratch_shapes=[pltpu.VMEM((total, rows, LANES), jnp.float32)],
        compiler_params=params(),
    )(origin, *parts)


def products_of(flat, cluster):
    return lax.dot_general(
        flat, cluster, (((1,), (1,)), ((), ())), preferred_element_type=jnp.float32
    )


def weigh(products, norms):
    scores = (products - norms) * INV_WIDTH
    row_top = jnp.max(scores, axis=1, keepdims=True)
    weights = jnp.exp(scores - row_top)
    totals = jnp.sum(weights, axis=1, keepdims=True)
    log_weight = row_top + jnp.log(totals)
    first = log_weight.astype(jnp.bfloat16).astype(jnp.float32)
    rest = log_weight - first
    second = rest.astype(jnp.bfloat16).astype(jnp.float32)
    third = rest - second
    lane = lax.broadcasted_iota(jnp.int32, (products.shape[0], LANES), 1) % TERM_LANES
    terms = jnp.where(lane == 0, first, jnp.where(lane == 1, second, third))
    return weights.astype(jnp.bfloat16), totals, terms


def score_kernel(*refs):
    count = len(GROUPS)
    part_refs, refs = refs[:count], refs[count:]
    (own_ref, *cluster_anys), refs = refs[:count], refs[count:]
    norm_refs, refs = refs[:count], refs[count:]
    out_refs, (clusters_ref, cluster_sems) = refs[:count], refs[count:]
    copies = [
        pltpu.make_async_copy(cluster_any, clusters_ref.at[index], cluster_sems.at[index])
        for index, cluster_any in enumerate(cluster_anys)
    ]
    for copy in copies:
        copy.start()
    size, rows, features = part_refs[0].shape
    half = size // 2

    def cluster_rows(cluster):
        return own_ref[...] if cluster == OWN else clusters_ref[cluster - 1]

    lines = half * rows
    first_half = lax.broadcasted_iota(jnp.int32, (rows, LANES), 1) < LANES // 2
    members = [
        [(group, side) for group, pair in enumerate(GROUPS) for side in range(2) if pair[side] == cluster]
        for cluster in range(count)
    ]
    products = []
    for cluster in range(count):
        flat = jnp.concatenate(
            [
                part_refs[group][side * half : (side + 1) * half]
                .astype(jnp.float32)
                .reshape(lines, features)
                for group, side in members[cluster]
            ]
        ).astype(jnp.bfloat16)
        if cluster != OWN:
            copies[cluster - 1].wait()
        products.append(products_of(flat, cluster_rows(cluster)))
    for cluster in range(count):
        weights, totals, terms = weigh(products[cluster], norm_refs[cluster][...])
        summed = jnp.dot(weights, cluster_rows(cluster), preferred_element_type=jnp.float32)
        part = summed * (1.0 / totals)
        for place, (group, side) in enumerate(members[cluster]):
            first, out_ref = place * lines, out_refs[group]
            out_ref[side * half : (side + 1) * half] = (
                part[first : first + lines].reshape(half, rows, features).astype(jnp.bfloat16)
            )
            for index in range(0, half, 2):
                line = first + index * rows
                both = jnp.where(
                    first_half, terms[line : line + rows], terms[line + rows : line + 2 * rows]
                )
                lanes = (side * half + index) // 2 * LANES
                out_ref[size, :, lanes : lanes + LANES] = both.astype(jnp.bfloat16)


def score_parts(parts, clusters, norms):
    count = len(GROUPS)
    size, rows, features = parts[0].shape
    references = clusters[0].shape[0]
    total = count * size * rows
    out = jax.ShapeDtypeStruct((size + 1, rows, features), jnp.bfloat16)
    return pl.pallas_call(
        score_kernel,
        out_shape=[out] * count,
        in_specs=[VMEM] * (count + 1) + [whole(pl.ANY)] * (count - 1) + [VMEM] * count,
        out_specs=[VMEM] * count,
        scratch_shapes=[
            pltpu.VMEM((count - 1, references, features), jnp.bfloat16),
            pltpu.SemaphoreType.DMA((count - 1,)),
        ],
        compiler_params=params(),
        cost_estimate=pl.CostEstimate(
            flops=4 * total * references * features,
            bytes_accessed=2 * (2 * total * features + count * references * features),
            transcendentals=total * references,
        ),
    )(*parts, *clusters, *norms)


def combine_kernel(log_count, step, slots_ref, squares_ref, returned_ref, earlier_ref, *out_refs):
    density_ref, *out_refs = out_refs
    rows = squares_ref.shape[0]
    count = slots_ref.shape[0] // 2
    per_slab = 2 * count // SLABS
    tiles = (returned_ref.shape[0] // SLABS - 1) // per_slab
    row = lax.broadcasted_iota(jnp.int32, (rows, LANES), 0)
    lane = lax.broadcasted_iota(jnp.int32, (rows, LANES), 1)
    lane_slot = jnp.where(
        lane % TERM_LANES < TERMS, lane % (LANES // 2) // TERM_LANES, -1
    )
    last = len(out_refs) == 1
    squares = squares_ref[...]

    def read(slot):
        base, shared, rank = chunk_base(slot, per_slab, tiles)
        part = returned_ref[pl.ds(base, tiles)].astype(jnp.float32)
        terms = returned_ref[shared].astype(jnp.float32)
        terms = jnp.where(lane_slot == rank, terms, 0.0)
        return part, jnp.sum(terms, axis=1, keepdims=True)

    def body(block, carry):
        densities, next_squares = carry
        first_slot, second_slot = slots_ref[2 * block], slots_ref[2 * block + 1]
        first_part, first_log = read(first_slot)
        second_part, second_log = read(second_slot)
        both_top = jnp.maximum(first_log, second_log)
        first_share = jnp.exp(first_log - both_top)
        second_share = jnp.exp(second_log - both_top)
        pair_total = first_share + second_share
        inverse = 1.0 / pair_total
        mixed = (
            (first_share * inverse)[None] * first_part
            + (second_share * inverse)[None] * second_part
        ).astype(jnp.bfloat16)
        density = both_top + jnp.log(pair_total)
        densities = jnp.where(lane == block, density, densities)
        if last:
            for tile in range(tiles):
                out_refs[0][block, :, tile * LANES : (tile + 1) * LANES] = mixed[tile]
            return densities, next_squares
        for tile in range(tiles):
            lanes = slice(tile * LANES, (tile + 1) * LANES)
            out_refs[0][first_slot, :, lanes] = mixed[tile]
            out_refs[0][second_slot, :, lanes] = mixed[tile]
        total = jnp.sum(jnp.square(mixed.astype(jnp.float32)), axis=0)
        total = jnp.sum(total, axis=1, keepdims=True)
        return densities, jnp.where(lane == block, total, next_squares)

    zeros = jnp.zeros((rows, LANES), jnp.float32)
    densities, next_squares = lax.fori_loop(0, count, body, (zeros, zeros), unroll=32)
    if not last:
        out_refs[1][...] = next_squares
    densities = densities - 0.5 * INV_WIDTH * squares - log_count
    blocks_wide = LANES // rows
    for wide in range(count // blocks_wide):
        spread = zeros
        for index in range(blocks_wide):
            block = wide * blocks_wide + index
            column = densities[:, block : block + 1]
            spread = jnp.where(lane == index * rows + row, column, spread)
        line = jnp.sum(
            jnp.where(lane % rows == row, spread, 0.0), axis=0, keepdims=True
        )
        lanes = slice(wide * LANES, (wide + 1) * LANES)
        for other in range(density_ref.shape[0]):
            if other == step:
                density_ref[other : other + 1, lanes] = line
            else:
                density_ref[other : other + 1, lanes] = earlier_ref[other : other + 1, lanes]


def combine(squares, returned, slots, earlier, log_count, step, features):
    rows = squares.shape[0]
    total = slots.shape[0]
    outs = [jax.ShapeDtypeStruct(earlier.shape, jnp.float32)]
    if step == STEPS - 1:
        outs.append(jax.ShapeDtypeStruct((total // 2, rows, features), jnp.bfloat16))
    else:
        outs.append(jax.ShapeDtypeStruct((total, rows, features), jnp.bfloat16))
        outs.append(jax.ShapeDtypeStruct(squares.shape, jnp.float32))
    return pl.pallas_call(
        functools.partial(combine_kernel, log_count, step),
        out_shape=outs,
        in_specs=[SMEM, VMEM, VMEM, VMEM],
        out_specs=[VMEM] * len(outs),
        compiler_params=params(),
    )(slots, squares, returned, earlier)


def half_norms_of(cluster_rows):
    return 0.5 * jnp.sum(jnp.square(cluster_rows.astype(jnp.float32)), axis=1)[None, :]


def sorted_origins(arrived, total, depth, core):
    chunks = arrived.reshape(SLABS, -1, *arrived.shape[1:])
    targets = chunks[:, -1, 0, : total // SLABS].reshape(-1).astype(jnp.int32)
    order = jnp.arange(total, dtype=jnp.int32)
    earlier = (targets[:, None] == targets[None, :]) & (order[None, :] < order[:, None])
    rank = jnp.sum(earlier.astype(jnp.int32), axis=1)
    side = (targets % CORES) ^ core
    ahead = targets // CORES - depth
    ahead = jnp.where(core == 0, ahead, -ahead) % DEPTH
    half = sum(
        jnp.where((side == at) & (ahead == steps), HALVES[at][steps], 0)
        for at in range(CORES)
        for steps in range(DEPTH)
    )
    slot = half * (total // CLUSTER_DEVICES) + rank
    return jnp.sum(jnp.where(slot[None, :] == order[:, None], order[None, :], 0), axis=1)


def local(queries, corpus, block_pairs, owner_table):
    features = queries.shape[2]
    cluster_index = lax.axis_index("cluster").astype(jnp.int32)
    depth, core = cluster_index // CORES, cluster_index % CORES
    own = corpus[0]
    ahead = send_ahead(own, -1)
    other = swap_cores(own)
    log_count = math.log(2.0 * own.shape[0])
    outgoing, slots, squares = fill(queries, block_pairs.T, owner_table)
    densities = jnp.zeros((STEPS, queries.shape[0] * queries.shape[1]), jnp.float32)
    for step in range(STEPS):
        arrived = exchange_slabs(outgoing)
        if step == 0:
            origin = sorted_origins(arrived, slots.shape[0], depth, core)
        parts = list(sort_by_depth(arrived, origin, features))
        if step == 0:
            ahead, parts[0] = lax.optimization_barrier((ahead, parts[0]))
            clusters = (own, other, ahead, swap_cores(ahead))
            norms = [half_norms_of(cluster) for cluster in clusters]
        parts[STAY:] = [send_ahead(parts[STAY], 1), send_ahead(parts[STAY + 1], -1)]
        answers = list(score_parts(parts, clusters, norms))
        answers[STAY:] = [send_ahead(answers[STAY], -1), send_ahead(answers[STAY + 1], 1)]
        returned = exchange_slabs(unsort(answers, origin))
        densities, outgoing, *squares_next = combine(
            squares, returned, slots, densities, log_count, step, features
        )
        squares = squares_next[0] if squares_next else None
    return (outgoing, densities)


def solution(mesh):
    return jax.shard_map(
        local,
        mesh=mesh,
        in_specs=(
            P(("cluster", "slab"), None, None),
            P(("cluster", "slab"), None, None),
            P(("cluster", "slab"), None),
            P(),
        ),
        out_specs=(P(("cluster", "slab"), None, None), P(None, ("cluster", "slab"))),
        check_vma=False,
    )
```
